256 devices in a mesh: row: 8 (over z_hi, core), col: 32 (over z_lo, y, x).
Axes of the slice: x: 4, y: 4, z: 8 (z_hi: 4, z_lo: 2; z = z_hi * 2 + z_lo), core: 2. Of those that a mesh axis runs over, the one named last changes fastest.
Arguments:
- pair_rep: bfloat16 [2048, 2048, 128], P('row', 'col'), may hold values from -6 to 6
- ln_in_gain: float32 [128], replicated, may hold values from 0.1 to 1.9
- ln_in_bias: float32 [128], replicated, may hold values from -3 to 3
- w_left_gate: bfloat16 [128, 128], replicated, may hold values from -0.5 to 0.5
- w_left_proj: bfloat16 [128, 128], replicated, may hold values from -0.5 to 0.5
- w_right_gate: bfloat16 [128, 128], replicated, may hold values from -0.5 to 0.5
- w_right_proj: bfloat16 [128, 128], replicated, may hold values from -0.5 to 0.5
- w_out_gate: bfloat16 [128, 128], replicated, may hold values from -0.5 to 0.5
- ln_out_gain: float32 [128], replicated, may hold values from 0.1 to 1.9
- ln_out_bias: float32 [128], replicated, may hold values from -3 to 3
- w_output: bfloat16 [128, 128], replicated, may hold values from -0.5 to 0.5
Outputs:
- update: bfloat16 [2048, 2048, 128], P('row', 'col')
The draws below stay inside these ranges and needn't reach their ends.
All inputs are finite; a program needn't handle non-finite values.
Results may differ from the reference program's by a relative error of at most 0.0055.
Values may be sent and summed in bfloat16 or wider, within the bound.
A program may use at most 128 MiB of HBM per device.

```python
import jax
import jax.numpy as jnp
from jax import lax

C = 128
N = 2048
KD = 6
N_ROW = 8
N_COL = 32


def shard_levels(stream_key, dims, cuts, smallest, high):
    def one(dim, blocks):
        heights = jax.random.uniform(jax.random.fold_in(jax.random.fold_in(stream_key, 6), dim), (blocks,), jnp.float32, smallest / len(cuts), high / len(cuts))
        return jnp.repeat(jnp.exp(heights), dims[dim] // blocks).reshape((-1,) + (1,) * (len(dims) - dim - 1))

    level = one(*cuts[0])
    for cut in cuts[1:]:
        level = level * one(*cut)
    return level


def bell_draw(own_key, extent, scale, most, cuts=(), kind=jnp.bfloat16):
    level = shard_levels(own_key, extent, cuts, -0.22, 0.18) if cuts else 1.0
    values = jax.random.normal(own_key, extent, jnp.float32) * scale * level
    return jnp.minimum(jnp.maximum(values, -most), most).astype(kind)


def setup_inputs(seed: int = 0) -> dict:
    splits = jax.random.split(jax.random.key(seed), 12)
    return {
        "pair_rep": bell_draw(splits[0], (N, N, C), 1.0, 6.0, ((0, 8), (1, 32))),
        "ln_in_gain": jnp.clip(1.0 + 0.18 * jax.random.normal(splits[1], (C,), jnp.float32), 0.1, 1.9),
        "ln_in_bias": bell_draw(splits[2], (C,), 0.5, 3.0, (), jnp.float32),
        "w_left_gate": bell_draw(splits[3], (C, C), C ** -0.5, 0.5),
        "w_left_proj": bell_draw(splits[4], (C, C), C ** -0.5, 0.5),
        "w_right_gate": bell_draw(splits[5], (C, C), C ** -0.5, 0.5),
        "w_right_proj": bell_draw(splits[6], (C, C), C ** -0.5, 0.5),
        "w_out_gate": bell_draw(splits[7], (C, C), C ** -0.5, 0.5),
        "ln_out_gain": jnp.clip(1.0 + 0.18 * jax.random.normal(splits[8], (C,), jnp.float32), 0.1, 1.9),
        "ln_out_bias": bell_draw(splits[9], (C,), 0.5, 3.0, (), jnp.float32),
        "w_output": bell_draw(splits[10], (C, C), C ** -0.5, 0.5),
    }


def layer_norm(values, gain, bias):
    mean_val = lax.optimization_barrier(jnp.mean(values, axis=-1, keepdims=True))
    centred = values - mean_val
    spread = lax.optimization_barrier(jnp.mean(centred * centred, axis=-1, keepdims=True))
    return centred * lax.rsqrt(spread + 1e-05) * gain + bias

def gated_panel(window, w_gate, w_proj):
    gate_part = jnp.dot(window, w_gate, preferred_element_type=jnp.float32)
    value_part = jnp.dot(window, w_proj, preferred_element_type=jnp.float32)
    return (jax.nn.sigmoid(gate_part) * value_part).astype(jnp.bfloat16)

def reference(pair_rep, ln_in_gain, ln_in_bias, w_left_gate, w_left_proj, w_right_gate, w_right_proj, w_out_gate, ln_out_gain, ln_out_bias, w_output):
    channels = pair_rep.shape[2]
    tile_cols = N // N_COL
    tile_rows = N // N_ROW
    columns = pair_rep.reshape(N, N_COL, tile_cols, channels)[:, :, :KD, :].reshape(N, KD * N_COL, channels)
    window = layer_norm(columns.astype(jnp.float32), ln_in_gain, ln_in_bias).astype(jnp.bfloat16)
    left_panel = gated_panel(window, w_left_gate, w_left_proj)
    right_panel = gated_panel(window, w_right_gate, w_right_proj).astype(jnp.float32)
    pair_blocks = pair_rep.reshape(N_ROW, tile_rows, N, channels)
    left_blocks = left_panel.reshape(N_ROW, tile_rows, KD * N_COL, channels)

    def one_block(inputs):
        pair_block, left_block = inputs
        product = jnp.einsum('ikc,jkc->ijc', left_block.astype(jnp.float32), right_panel)
        mixed = layer_norm(product, ln_out_gain, ln_out_bias).astype(jnp.bfloat16)
        normed = layer_norm(pair_block.astype(jnp.float32), ln_in_gain, ln_in_bias).astype(jnp.bfloat16)
        gate = jax.nn.sigmoid(jnp.dot(normed, w_out_gate, preferred_element_type=jnp.float32))
        projected = jnp.dot(mixed, w_output, preferred_element_type=jnp.float32)
        return (gate * projected).astype(jnp.bfloat16)
    update = lax.map(one_block, (pair_blocks, left_blocks))
    return update.reshape(N, N, channels)
```

```python
import functools

import jax
import jax.numpy as jnp
from jax import lax
from jax.experimental import pallas as pl
from jax.experimental.pallas import tpu as pltpu
from jax.sharding import PartitionSpec as P

MESH = pl.DeviceIdType.MESH
F32 = jnp.float32
BF16 = jnp.bfloat16
NK = 6
DF = (0, -1, 1, 2)
N_COPIES = 84


def norm_rows(x, gain, bias):
    average = jnp.full((128, 128), 1.0 / 128, BF16)
    centred = x.astype(F32) - jnp.dot(x, average, preferred_element_type=F32)
    spread = jnp.dot((centred * centred).astype(BF16), average, preferred_element_type=F32)
    return (centred * lax.rsqrt(spread + 1e-05) * gain + bias).astype(BF16)


def kernel(
    z_hbm, gin_ref, bin_ref, wlg_ref, wlp_ref, wrg_ref, wrp_ref, wog_ref, gout_ref, bout_ref, wo_ref,
    out_hbm,
    zv, zf, wt, normed_w, panel, r_send, r_gather, r_nat, r_mat, lefts, swap, acc, proj, gain_c, bias_c,
    z_sem, out_sem, send_sem, recv_sem, r1_send, r1_recv, r2_send, r2_recv, rf_send, rf_recv, r3_send, r3_recv,
):
    row, col = lax.axis_index("row"), lax.axis_index("col")
    zh, core = row // 2, row % 2
    zl, y, x = col // 16, (col // 4) % 4, col % 4

    def dev(zh_=None, core_=None, zl_=None, y_=None, x_=None):
        a = zh if zh_ is None else zh_
        b = core if core_ is None else core_
        c = zl if zl_ is None else zl_
        d = y if y_ is None else y_
        e = x if x_ is None else x_
        return (a * 2 + b, c * 16 + d * 4 + e)

    barrier = pltpu.get_barrier_semaphore()

    def greet(target):
        pl.semaphore_signal(barrier, inc=1, device_id=target, device_id_type=MESH)

    for n in range(1, 16):
        p = (y * 4 + x + n) % 16
        greet(dev(y_=p // 4, x_=p % 4))
    for n in range(1, 8):
        p = (zh * 2 + zl + n) % 8
        greet(dev(zh_=p // 2, zl_=p % 2))
    greet(dev(core_=1 - core))

    head = pltpu.make_async_copy(z_hbm.at[:, pl.ds(0, 16), :], zv.at[:, pl.ds(0, 16), :], z_sem.at[0])
    rest = pltpu.make_async_copy(z_hbm.at[:, pl.ds(16, 48), :], zv.at[:, pl.ds(16, 48), :], z_sem.at[1])
    head.start()
    rest.start()

    gin, bias_in = gin_ref[...].reshape(1, 128), bin_ref[...].reshape(1, 128)
    for n, w in enumerate((wlg_ref, wlp_ref, wrg_ref, wrp_ref)):
        wt[n * 128 : (n + 1) * 128, :] = w[...].astype(F32).T.astype(BF16)
    gain_c[...] = jnp.broadcast_to(gout_ref[...].reshape(1, 128), (128, 128)).T
    bias_c[...] = jnp.broadcast_to(bout_ref[...].reshape(1, 128), (128, 128)).T

    head.wait()

    def widen(b, _):
        i0 = pl.multiple_of(b * 8, 8)
        v = zv[pl.ds(i0, 8), 0:16, :].astype(F32)
        for i in range(8):
            zf[pl.ds((i0 + i) * 9, 8), :] = v[i, 0:8]
        return 0

    lax.fori_loop(0, 32, widen, 0, unroll=4)

    def norm_window(k, _):
        v = zf[pl.ds(k, 256, stride=9), :].astype(BF16)
        normed_w[k] = norm_rows(v, gin, bias_in)
        return 0

    lax.fori_loop(0, NK, norm_window, 0, unroll=3)

    def project(k, part):
        return lax.dot_general(
            wt[part * 256 : part * 256 + 256, :], normed_w[k], (((1,), (1,)), ((), ())), preferred_element_type=F32
        )

    def window_left(k, _):
        both = project(k, 0)
        left = (jax.nn.sigmoid(both[0:128]) * both[128:256]).astype(BF16)
        for h in range(2):
            for ab in range(2):
                pair = (y * 4 + x) if ab == 0 else (x * 4 + y)
                panel[h, ab, pair, zl * NK + k] = left[ab * 64 : ab * 64 + 64, h * 128 : h * 128 + 128]
        return 0

    low = lax.broadcasted_iota(jnp.int32, (32, 128), 1) < 64

    def window_right(k, _):
        both = project(k, 1)
        right = jax.nn.sigmoid(both[0:128]) * both[128:256]
        for u in range(2):
            for ab in range(2):
                lo = right[ab * 64 : ab * 64 + 32, u * 128 : u * 128 + 128]
                hi = right[ab * 64 + 32 : ab * 64 + 64, u * 128 : u * 128 + 128]
                r_send[2 * u, k, ab * 32 : ab * 32 + 32, :] = jnp.where(low, lo, pltpu.roll(hi, 64, 1)).astype(BF16)
                r_send[2 * u + 1, k, ab * 32 : ab * 32 + 32, :] = jnp.where(low, pltpu.roll(lo, 64, 1), hi).astype(BF16)
        return 0

    lax.fori_loop(0, NK, window_right, 0, unroll=3)
    pl.semaphore_wait(barrier, 23)

    count = [0]
    copies = {}

    def left_copy(name, ref, target):
        n = count[0]
        count[0] += 1
        c = pltpu.make_async_remote_copy(
            src_ref=ref, dst_ref=ref, send_sem=send_sem.at[n], recv_sem=recv_sem.at[n], device_id=target, device_id_type=MESH
        )
        c.start()
        copies[name] = (n, c)

    def arrived(name, ref):
        n, _ = copies[name]
        pltpu.make_async_copy(ref, ref, recv_sem.at[n]).wait()

    def first(ab):
        return x if ab == 0 else y

    def second(ab):
        return y if ab == 0 else x

    def step_first(ab, d):
        return dev(x_=(x + d) % 4) if ab == 0 else dev(y_=(y + d) % 4)

    def step_second(ab, d):
        return dev(y_=(y + d) % 4) if ab == 0 else dev(x_=(x + d) % 4)

    def pair_ref(h, ab, ds, df, half=None):
        p = ((second(ab) + ds) % 4) * 4 + (first(ab) + df) % 4
        if half is None:
            return panel.at[h, ab, p]
        return panel.at[h, ab, p, :, pl.ds(half * 32, 32), :]

    def z_ref(h, ab, z):
        return panel.at[h, ab, second(ab) * 4 + first(ab), pl.ds(z * NK, NK)]

    def send_z(h):
        for ab in range(2):
            left_copy(("z", h, ab), z_ref(h, ab, zl), dev(zl_=1 - zl))

    def wait_z(h):
        for ab in range(2):
            arrived(("z", h, ab), z_ref(h, ab, 1 - zl))

    def send_p1(h):
        for ab in range(2):
            for d in (1, -1):
                left_copy(("p1", h, ab, d), pair_ref(h, ab, 0, 0), step_first(ab, d))

    def send_q1(h, df):
        for ab in range(2):
            for d in (1, -1):
                left_copy(("q1", h, ab, df, d), pair_ref(h, ab, 0, df), step_second(ab, d))

    def pass_p1(h):
        for d in (1, -1):
            for ab in range(2):
                arrived(("p1", h, ab, d), pair_ref(h, ab, 0, -d))
                half = 0 if d == 1 else 1
                left_copy(("p2", h, ab, d), pair_ref(h, ab, 0, -d, half), step_first(ab, d))

    def wait_p2(h):
        for d in (1, -1):
            for ab in range(2):
                half = 0 if d == 1 else 1
                arrived(("p2", h, ab, d), pair_ref(h, ab, 0, 2, half))

    def pass_q1(h, df):
        for d in (1, -1):
            for ab in range(2):
                arrived(("q1", h, ab, df, d), pair_ref(h, ab, -d, df))
                half = 0 if d == 1 else 1
                left_copy(("q2", h, ab, df, d), pair_ref(h, ab, -d, df, half), step_second(ab, d))

    def wait_q2(h, df):
        for d in (1, -1):
            for ab in range(2):
                half = 0 if d == 1 else 1
                arrived(("q2", h, ab, df, d), pair_ref(h, ab, 2, df, half))

    own_slot = y * 4 + x
    ty = row % 4
    gathers = jnp.logical_and(y // 2 == zh % 2, core == y % 2)
    relays = core == y % 2

    def r1_ref(ref, n, ab):
        return ref.at[n, :, pl.ds(ab * 32, 32), :]

    def r1_copy(q, ab):
        return pltpu.make_async_remote_copy(
            src_ref=r1_ref(r_send, q, ab), dst_ref=r1_ref(r_gather, own_slot, ab),
            send_sem=r1_send.at[q * 2 + ab], recv_sem=r1_recv.at[ab], device_id=dev(y_=ty, x_=q), device_id_type=MESH,
        )

    def r1_mine(q):
        return jnp.logical_and(ty == y, x == q)

    def start_r1():
        for ab in range(2):
            for q in range(4):
                @pl.when(r1_mine(q))
                def _():
                    pltpu.make_async_copy(r1_ref(r_send, q, ab), r1_ref(r_gather, own_slot, ab), r1_recv.at[ab]).start()

                @pl.when(jnp.logical_not(r1_mine(q)))
                def _():
                    r1_copy(q, ab).start()

    def piece(ref, p):
        return ref.at[:, :, pl.ds(p * 16, 16), :]

    def r2_copy(p, o):
        return pltpu.make_async_remote_copy(
            src_ref=piece(r_gather, p), dst_ref=piece(r_nat.at[zl], p), send_sem=r2_send.at[p * 4 + o],
            recv_sem=r2_recv.at[p * 2 + zl], device_id=dev(zh_=(zh + o) % 4, zl_=zh // 2), device_id_type=MESH,
        )

    at_home = zl == zh // 2

    def start_r2(ab):
        @pl.when(gathers)
        def _():
            got = r_gather.at[:, :, pl.ds(ab * 32, 32), :]
            pltpu.make_async_copy(got, got, r1_recv.at[ab]).wait()
            for p in (2 * ab, 2 * ab + 1):
                r2_copy(p, 1).start()
                r2_copy(p, 3).start()

                @pl.when(at_home)
                def _():
                    pltpu.make_async_copy(piece(r_gather, p), piece(r_nat.at[zl], p), r2_recv.at[p * 2 + zl]).start()

                @pl.when(jnp.logical_not(at_home))
                def _():
                    r2_copy(p, 0).start()

    rel = (zh + 4 - (2 * zl + y // 2)) % 4

    def far_ref(p, z, half):
        return r_nat.at[z, pl.ds(half * 8, 8), :, pl.ds(p * 16, 16), :]

    def far_copy(p, z, half):
        return pltpu.make_async_remote_copy(
            src_ref=far_ref(p, z, half), dst_ref=far_ref(p, z, half), send_sem=rf_send.at[p * 2 + z],
            recv_sem=rf_recv.at[p * 4 + z * 2 + half],
            device_id=dev(zh_=(zh + (1 if half == 0 else 3)) % 4), device_id_type=MESH,
        )

    def r3_copy(p, z):
        part = piece(r_nat.at[z], p)
        return pltpu.make_async_remote_copy(
            src_ref=part, dst_ref=part, send_sem=r3_send.at[p * 2 + z], recv_sem=r3_recv.at[p * 2 + z],
            device_id=dev(core_=1 - core), device_id_type=MESH,
        )

    def pass_r2(p):
        @pl.when(jnp.logical_and(relays, rel != 2))
        def _():
            for z in range(2):
                part = piece(r_nat.at[z], p)
                pltpu.make_async_copy(part, part, r2_recv.at[p * 2 + z]).wait()
                for half in range(2):
                    @pl.when(rel == 1 + 2 * half)
                    def _():
                        far_copy(p, z, half).start()
                r3_copy(p, z).start()

    def wait_right(p):
        @pl.when(jnp.logical_and(relays, rel == 2))
        def _():
            for z in range(2):
                for half in range(2):
                    part = far_ref(p, z, half)
                    pltpu.make_async_copy(part, part, rf_recv.at[p * 4 + z * 2 + half]).wait()
                r3_copy(p, z).start()

        @pl.when(jnp.logical_not(relays))
        def _():
            for z in range(2):
                part = piece(r_nat.at[z], p)
                pltpu.make_async_copy(part, part, r3_recv.at[p * 2 + z]).wait()

    def gate_part(lo, hi):
        def body(b, _):
            i0 = pl.multiple_of(b * 4, 4)
            normed = norm_rows(zv[pl.ds(i0, 4)].reshape(256, 128), gin, bias_in)
            g = jax.nn.sigmoid(jnp.dot(normed, wog_ref[...], preferred_element_type=F32))
            zv[pl.ds(i0, 4)] = g.astype(BF16).reshape(4, 64, 128)
            return 0

        lax.fori_loop(lo, hi, body, 0, unroll=4)

    def prep_right(p):
        ab = p // 2

        def relay(s, _):
            for f in range(4):
                slot_ = (s * 4 + f) if ab == 0 else (f * 4 + s)
                for z in range(2):
                    for k in range(NK):
                        zf[pl.ds(s * 48 + f * 12 + z * NK + k, 16, stride=193), :] = r_nat[
                            z, slot_, k, p * 16 : p * 16 + 16, :
                        ].astype(F32)
            return 0

        lax.fori_loop(0, 4, relay, 0)

        def turn(c, _):
            m = zf[pl.ds(c * 193, 192), :]
            r_mat[p * 16 + c] = m.astype(BF16).T
            return 0

        lax.fori_loop(0, 16, turn, 0, unroll=4)

    def relayout(h, ds):
        for ab in range(2):
            s = (second(ab) + ds) % 4

            def relay(f, _):
                for k in range(2 * NK):
                    rows = pl.ds(f * 12 + k, 64, stride=49)
                    swap[ab, rows, :] = panel[h, ab, s * 4 + f, k].astype(F32)
                return 0

            lax.fori_loop(0, 4, relay, 0)

            def pack(c, _):
                v = swap[ab, pl.ds(c * 49, 48), :]
                lefts[h, ab * 64 + c, pl.ds(pl.multiple_of(s * 48, 16), 48), :] = v.astype(BF16)
                return 0

            lax.fori_loop(0, 64, pack, 0, unroll=8)

    def multiply(h, p):
        def mul(n, _):
            c2 = p * 16 + n
            for cp in range(2):
                c = (p // 2) * 64 + cp * 32 + (p % 2) * 16 + n
                part = jnp.dot(r_mat[c2, cp * 64 : cp * 64 + 64, :], lefts[h, c], preferred_element_type=F32)
                acc[pl.ds(c * 65, 64), :] = part
            return 0

        lax.fori_loop(0, 16, mul, 0, unroll=4)

    def finish(h):
        def column(j, _):
            p = acc[pl.ds(j, 128, stride=65), :]
            mean = jnp.mean(p, axis=0, keepdims=True)
            centred = p - mean
            spread = jnp.mean(centred * centred, axis=0, keepdims=True)
            mixed = centred * lax.rsqrt(spread + 1e-05) * gain_c[...] + bias_c[...]
            turned = mixed.astype(BF16).T
            proj[pl.ds(j, 128, stride=65), :] = jnp.dot(turned, wo_ref[...], preferred_element_type=F32)
            return 0

        lax.fori_loop(0, 64, column, 0, unroll=4)

        for part in range(4):
            def body(i, _):
                g = zv[h * 128 + i].astype(F32)
                v = g * proj[pl.ds(i * 65, 64), :]
                zv[h * 128 + i] = v.astype(BF16)
                return 0

            lax.fori_loop(part * 32, part * 32 + 32, body, 0, unroll=8)
            out_copy(h, part).start()

    def out_copy(h, part):
        rows = pl.ds(h * 128 + part * 32, 32)
        return pltpu.make_async_copy(zv.at[rows], out_hbm.at[rows], out_sem.at[h * 4 + part])

    start_r1()
    lax.fori_loop(0, NK, window_left, 0, unroll=3)
    send_z(0)
    send_z(1)
    rest.wait()
    gate_part(0, 4)
    wait_z(0)
    send_p1(0)
    send_q1(0, 0)
    gate_part(4, 8)
    start_r2(0)
    gate_part(8, 12)
    pass_p1(0)
    send_q1(0, -1)
    send_q1(0, 1)
    start_r2(1)
    gate_part(12, 20)
    pass_q1(0, 0)
    wait_p2(0)
    send_q1(0, 2)
    gate_part(20, 28)
    wait_z(1)
    send_p1(1)
    relayout(0, 0)
    gate_part(28, 36)
    pass_q1(0, -1)
    pass_q1(0, 1)
    send_q1(1, 0)
    gate_part(36, 44)
    pass_r2(0)
    gate_part(44, 48)
    pass_q1(0, 2)
    pass_p1(1)
    send_q1(1, -1)
    send_q1(1, 1)
    gate_part(48, 56)
    pass_r2(1)
    gate_part(56, 64)
    relayout(0, -1)
    pass_q1(1, 0)
    wait_p2(1)
    send_q1(1, 2)
    pass_r2(2)
    relayout(0, 1)
    for df in DF:
        wait_q2(0, df)
    relayout(0, 2)
    pass_r2(3)
    pass_q1(1, -1)
    pass_q1(1, 1)
    wait_right(0)
    prep_right(0)
    multiply(0, 0)
    wait_right(1)
    prep_right(1)
    multiply(0, 1)
    relayout(1, 0)
    wait_right(2)
    prep_right(2)
    multiply(0, 2)
    pass_q1(1, 2)
    wait_right(3)
    prep_right(3)
    multiply(0, 3)
    finish(0)
    relayout(1, -1)
    relayout(1, 1)
    for df in DF:
        wait_q2(1, df)
    relayout(1, 2)
    for p in range(4):
        multiply(1, p)
    finish(1)

    for n, c in copies.values():
        c.wait_send()
    for q in range(4):
        @pl.when(jnp.logical_not(r1_mine(q)))
        def _():
            for ab in range(2):
                r1_copy(q, ab).wait_send()

    @pl.when(gathers)
    def _():
        for p in range(4):
            r2_copy(p, 1).wait_send()
            r2_copy(p, 3).wait_send()

        @pl.when(jnp.logical_not(at_home))
        def _():
            for p in range(4):
                r2_copy(p, 0).wait_send()

    @pl.when(relays)
    def _():
        for p in range(4):
            for z in range(2):
                for half in range(2):
                    @pl.when(rel == 1 + 2 * half)
                    def _():
                        far_copy(p, z, half).wait_send()
                r3_copy(p, z).wait_send()

    for h in range(2):
        for part in range(4):
            out_copy(h, part).wait()


def body(*args):
    vmem = pl.BlockSpec(memory_space=pltpu.VMEM)
    anywhere = pl.BlockSpec(memory_space=pl.ANY)
    return pl.pallas_call(
        kernel,
        out_shape=jax.ShapeDtypeStruct((256, 64, 128), BF16),
        in_specs=[anywhere] + [vmem] * 10,
        out_specs=anywhere,
        scratch_shapes=[
            pltpu.VMEM((256, 64, 128), BF16),
            pltpu.VMEM((3104, 128), F32),
            pltpu.VMEM((512, 128), BF16),
            pltpu.VMEM((NK, 256, 128), BF16),
            pltpu.VMEM((2, 2, 16, 12, 64, 128), BF16),
            pltpu.VMEM((4, NK, 64, 128), BF16),
            pltpu.VMEM((16, NK, 64, 128), BF16),
            pltpu.VMEM((2, 16, NK, 64, 128), BF16),
            pltpu.VMEM((64, 128, 192), BF16),
            pltpu.VMEM((2, 128, 192, 128), BF16),
            pltpu.VMEM((2, 64 * 49, 128), F32),
            pltpu.VMEM((128 * 65, 128), F32),
            pltpu.VMEM((128 * 65, 128), F32),
            pltpu.VMEM((128, 128), F32),
            pltpu.VMEM((128, 128), F32),
            pltpu.SemaphoreType.DMA((2,)),
            pltpu.SemaphoreType.DMA((8,)),
            pltpu.SemaphoreType.DMA((N_COPIES,)),
            pltpu.SemaphoreType.DMA((N_COPIES,)),
            pltpu.SemaphoreType.DMA((8,)),
            pltpu.SemaphoreType.DMA((2,)),
            pltpu.SemaphoreType.DMA((16,)),
            pltpu.SemaphoreType.DMA((8,)),
            pltpu.SemaphoreType.DMA((8,)),
            pltpu.SemaphoreType.DMA((16,)),
            pltpu.SemaphoreType.DMA((8,)),
            pltpu.SemaphoreType.DMA((8,)),
        ],
        compiler_params=pltpu.CompilerParams(
            collective_id=0, has_side_effects=True, vmem_limit_bytes=60 * 1024 * 1024
        ),
        cost_estimate=pl.CostEstimate(flops=2_000_000_000, bytes_accessed=8_400_000, transcendentals=2_000_000),
    )(*args)


def solution(mesh):
    in_specs = (P("row", "col", None),) + (P(),) * 10
    return jax.shard_map(body, mesh=mesh, in_specs=in_specs, out_specs=P("row", "col", None), check_vma=False)
```

```python
import functools

import jax
import jax.numpy as jnp
from jax import lax
from jax.experimental import pallas as pl
from jax.experimental.pallas import tpu as pltpu
from jax.sharding import PartitionSpec as P

MESH = pl.DeviceIdType.MESH
F32 = jnp.float32
BF16 = jnp.bfloat16
NK = 6
DF = (0, -1, 1, 2)
N_COPIES = 84


def norm_rows(x, gain, bias):
    average = jnp.full((128, 128), 1.0 / 128, BF16)
    centred = x.astype(F32) - jnp.dot(x, average, preferred_element_type=F32)
    spread = jnp.dot((centred * centred).astype(BF16), average, preferred_element_type=F32)
    return (centred * lax.rsqrt(spread + 1e-05) * gain + bias).astype(BF16)


def kernel(
    z_hbm, gin_ref, bin_ref, wlg_ref, wlp_ref, wrg_ref, wrp_ref, wog_ref, gout_ref, bout_ref, wo_ref,
    out_hbm,
    zv, zf, wt, normed_w, panel, r_send, r_gather, r_nat, r_mat, lefts, swap, acc, sums, proj, gain_c, bias_c,
    z_sem, out_sem, send_sem, recv_sem, r1_send, r1_recv, r2_send, r2_recv, rf_send, rf_recv, r3_send, r3_recv,
):
    row, col = lax.axis_index("row"), lax.axis_index("col")
    zh, core = row // 2, row % 2
    zl, y, x = col // 16, (col // 4) % 4, col % 4

    def dev(zh_=None, core_=None, zl_=None, y_=None, x_=None):
        a = zh if zh_ is None else zh_
        b = core if core_ is None else core_
        c = zl if zl_ is None else zl_
        d = y if y_ is None else y_
        e = x if x_ is None else x_
        return (a * 2 + b, c * 16 + d * 4 + e)

    barrier = pltpu.get_barrier_semaphore()

    def greet(target):
        pl.semaphore_signal(barrier, inc=1, device_id=target, device_id_type=MESH)

    for n in range(1, 16):
        p = (y * 4 + x + n) % 16
        greet(dev(y_=p // 4, x_=p % 4))
    for n in range(1, 8):
        p = (zh * 2 + zl + n) % 8
        greet(dev(zh_=p // 2, zl_=p % 2))
    greet(dev(core_=1 - core))

    head = pltpu.make_async_copy(z_hbm.at[:, pl.ds(0, 16), :], zv.at[:, pl.ds(0, 16), :], z_sem.at[0])
    rest = pltpu.make_async_copy(z_hbm.at[:, pl.ds(16, 48), :], zv.at[:, pl.ds(16, 48), :], z_sem.at[1])
    head.start()
    rest.start()

    gin, bias_in = gin_ref[...].reshape(1, 128), bin_ref[...].reshape(1, 128)
    for n, w in enumerate((wlg_ref, wlp_ref, wrg_ref, wrp_ref)):
        wt[n * 128 : (n + 1) * 128, :] = w[...].astype(F32).T.astype(BF16)
    gain_c[...] = jnp.broadcast_to(gout_ref[...].reshape(1, 128), (128, 128)).T
    bias_c[...] = jnp.broadcast_to(bout_ref[...].reshape(1, 128), (128, 128)).T

    head.wait()

    def widen(b, _):
        i0 = pl.multiple_of(b * 8, 8)
        v = zv[pl.ds(i0, 8), 0:16, :].astype(F32)
        for i in range(8):
            zf[pl.ds((i0 + i) * 9, 8), :] = v[i, 0:8]
        return 0

    lax.fori_loop(0, 32, widen, 0, unroll=4)

    def norm_window(k, _):
        v = zf[pl.ds(k, 256, stride=9), :].astype(BF16)
        normed_w[k] = norm_rows(v, gin, bias_in)
        return 0

    lax.fori_loop(0, NK, norm_window, 0, unroll=3)

    def project(k, part):
        return lax.dot_general(
            wt[part * 256 : part * 256 + 256, :], normed_w[k], (((1,), (1,)), ((), ())), preferred_element_type=F32
        )

    def window_left(k, _):
        both = project(k, 0)
        left = (jax.nn.sigmoid(both[0:128]) * both[128:256]).astype(BF16)
        for h in range(2):
            for ab in range(2):
                pair = (y * 4 + x) if ab == 0 else (x * 4 + y)
                panel[h, ab, pair, zl * NK + k] = left[ab * 64 : ab * 64 + 64, h * 128 : h * 128 + 128]
        return 0

    low = lax.broadcasted_iota(jnp.int32, (32, 128), 1) < 64

    def window_right(k, _):
        both = project(k, 1)
        right = jax.nn.sigmoid(both[0:128]) * both[128:256]
        for u in range(2):
            for ab in range(2):
                lo = right[ab * 64 : ab * 64 + 32, u * 128 : u * 128 + 128]
                hi = right[ab * 64 + 32 : ab * 64 + 64, u * 128 : u * 128 + 128]
                r_send[2 * u, k, ab * 32 : ab * 32 + 32, :] = jnp.where(low, lo, pltpu.roll(hi, 64, 1)).astype(BF16)
                r_send[2 * u + 1, k, ab * 32 : ab * 32 + 32, :] = jnp.where(low, pltpu.roll(lo, 64, 1), hi).astype(BF16)
        return 0

    lax.fori_loop(0, NK, window_right, 0, unroll=3)
    pl.semaphore_wait(barrier, 23)

    count = [0]
    copies = {}

    def left_copy(name, ref, target):
        n = count[0]
        count[0] += 1
        c = pltpu.make_async_remote_copy(
            src_ref=ref, dst_ref=ref, send_sem=send_sem.at[n], recv_sem=recv_sem.at[n], device_id=target, device_id_type=MESH
        )
        c.start()
        copies[name] = (n, c)

    def arrived(name, ref):
        n, _ = copies[name]
        pltpu.make_async_copy(ref, ref, recv_sem.at[n]).wait()

    def first(ab):
        return x if ab == 0 else y

    def second(ab):
        return y if ab == 0 else x

    def step_first(ab, d):
        return dev(x_=(x + d) % 4) if ab == 0 else dev(y_=(y + d) % 4)

    def step_second(ab, d):
        return dev(y_=(y + d) % 4) if ab == 0 else dev(x_=(x + d) % 4)

    def pair_ref(h, ab, ds, df, half=None):
        p = ((second(ab) + ds) % 4) * 4 + (first(ab) + df) % 4
        if half is None:
            return panel.at[h, ab, p]
        return panel.at[h, ab, p, :, pl.ds(half * 32, 32), :]

    def z_ref(h, ab, z):
        return panel.at[h, ab, second(ab) * 4 + first(ab), pl.ds(z * NK, NK)]

    def send_z(h):
        for ab in range(2):
            left_copy(("z", h, ab), z_ref(h, ab, zl), dev(zl_=1 - zl))

    def wait_z(h):
        for ab in range(2):
            arrived(("z", h, ab), z_ref(h, ab, 1 - zl))

    def send_p1(h):
        for ab in range(2):
            for d in (1, -1):
                left_copy(("p1", h, ab, d), pair_ref(h, ab, 0, 0), step_first(ab, d))

    def send_q1(h, df):
        for ab in range(2):
            for d in (1, -1):
                left_copy(("q1", h, ab, df, d), pair_ref(h, ab, 0, df), step_second(ab, d))

    def pass_p1(h):
        for d in (1, -1):
            for ab in range(2):
                arrived(("p1", h, ab, d), pair_ref(h, ab, 0, -d))
                half = 0 if d == 1 else 1
                left_copy(("p2", h, ab, d), pair_ref(h, ab, 0, -d, half), step_first(ab, d))

    def wait_p2(h):
        for d in (1, -1):
            for ab in range(2):
                half = 0 if d == 1 else 1
                arrived(("p2", h, ab, d), pair_ref(h, ab, 0, 2, half))

    def pass_q1(h, df):
        for d in (1, -1):
            for ab in range(2):
                arrived(("q1", h, ab, df, d), pair_ref(h, ab, -d, df))
                half = 0 if d == 1 else 1
                left_copy(("q2", h, ab, df, d), pair_ref(h, ab, -d, df, half), step_second(ab, d))

    def wait_q2(h, df):
        for d in (1, -1):
            for ab in range(2):
                half = 0 if d == 1 else 1
                arrived(("q2", h, ab, df, d), pair_ref(h, ab, 2, df, half))

    own_slot = y * 4 + x
    ty = row % 4
    gathers = jnp.logical_and(y // 2 == zh % 2, core == y % 2)
    relays = core == y % 2

    def r1_ref(ref, n, ab):
        return ref.at[n, :, pl.ds(ab * 32, 32), :]

    def r1_copy(q, ab):
        return pltpu.make_async_remote_copy(
            src_ref=r1_ref(r_send, q, ab), dst_ref=r1_ref(r_gather, own_slot, ab),
            send_sem=r1_send.at[q * 2 + ab], recv_sem=r1_recv.at[ab], device_id=dev(y_=ty, x_=q), device_id_type=MESH,
        )

    def r1_mine(q):
        return jnp.logical_and(ty == y, x == q)

    def start_r1():
        for ab in range(2):
            for q in range(4):
                @pl.when(r1_mine(q))
                def _():
                    pltpu.make_async_copy(r1_ref(r_send, q, ab), r1_ref(r_gather, own_slot, ab), r1_recv.at[ab]).start()

                @pl.when(jnp.logical_not(r1_mine(q)))
                def _():
                    r1_copy(q, ab).start()

    def piece(ref, p):
        return ref.at[:, :, pl.ds(p * 16, 16), :]

    def r2_copy(p, o):
        return pltpu.make_async_remote_copy(
            src_ref=piece(r_gather, p), dst_ref=piece(r_nat.at[zl], p), send_sem=r2_send.at[p * 4 + o],
            recv_sem=r2_recv.at[p * 2 + zl], device_id=dev(zh_=(zh + o) % 4, zl_=zh // 2), device_id_type=MESH,
        )

    at_home = zl == zh // 2

    def start_r2(ab):
        @pl.when(gathers)
        def _():
            got = r_gather.at[:, :, pl.ds(ab * 32, 32), :]
            pltpu.make_async_copy(got, got, r1_recv.at[ab]).wait()
            for p in (2 * ab, 2 * ab + 1):
                r2_copy(p, 1).start()
                r2_copy(p, 3).start()

                @pl.when(at_home)
                def _():
                    pltpu.make_async_copy(piece(r_gather, p), piece(r_nat.at[zl], p), r2_recv.at[p * 2 + zl]).start()

                @pl.when(jnp.logical_not(at_home))
                def _():
                    r2_copy(p, 0).start()

    rel = (zh + 4 - (2 * zl + y // 2)) % 4

    def far_ref(p, z, half):
        return r_nat.at[z, pl.ds(half * 8, 8), :, pl.ds(p * 16, 16), :]

    def far_copy(p, z, half):
        return pltpu.make_async_remote_copy(
            src_ref=far_ref(p, z, half), dst_ref=far_ref(p, z, half), send_sem=rf_send.at[p * 2 + z],
            recv_sem=rf_recv.at[p * 4 + z * 2 + half],
            device_id=dev(zh_=(zh + (1 if half == 0 else 3)) % 4), device_id_type=MESH,
        )

    def r3_copy(p, z):
        part = piece(r_nat.at[z], p)
        return pltpu.make_async_remote_copy(
            src_ref=part, dst_ref=part, send_sem=r3_send.at[p * 2 + z], recv_sem=r3_recv.at[p * 2 + z],
            device_id=dev(core_=1 - core), device_id_type=MESH,
        )

    def pass_r2(p):
        @pl.when(jnp.logical_and(relays, rel != 2))
        def _():
            for z in range(2):
                part = piece(r_nat.at[z], p)
                pltpu.make_async_copy(part, part, r2_recv.at[p * 2 + z]).wait()
                for half in range(2):
                    @pl.when(rel == 1 + 2 * half)
                    def _():
                        far_copy(p, z, half).start()
                r3_copy(p, z).start()

    def wait_right(p):
        @pl.when(jnp.logical_and(relays, rel == 2))
        def _():
            for z in range(2):
                for half in range(2):
                    part = far_ref(p, z, half)
                    pltpu.make_async_copy(part, part, rf_recv.at[p * 4 + z * 2 + half]).wait()
                r3_copy(p, z).start()

        @pl.when(jnp.logical_not(relays))
        def _():
            for z in range(2):
                part = piece(r_nat.at[z], p)
                pltpu.make_async_copy(part, part, r3_recv.at[p * 2 + z]).wait()

    def gate_part(lo, hi):
        def body(b, _):
            i0 = pl.multiple_of(b * 16, 16)
            normed = norm_rows(zv[pl.ds(i0, 16)].reshape(1024, 128), gin, bias_in)
            g = jax.nn.sigmoid(jnp.dot(normed, wog_ref[...], preferred_element_type=F32))
            zv[pl.ds(i0, 16)] = g.astype(BF16).reshape(16, 64, 128)
            return 0

        lax.fori_loop(lo // 4, hi // 4, body, 0)

    def prep_right(p):
        ab = p // 2

        def relay(s, _):
            for f in range(4):
                slot_ = (s * 4 + f) if ab == 0 else (f * 4 + s)
                for z in range(2):
                    for k in range(NK):
                        zf[pl.ds(s * 48 + f * 12 + z * NK + k, 16, stride=193), :] = r_nat[
                            z, slot_, k, p * 16 : p * 16 + 16, :
                        ].astype(F32)
            return 0

        lax.fori_loop(0, 4, relay, 0)

        def turn(c, _):
            m = zf[pl.ds(c * 193, 192), :]
            r_mat[p * 16 + c] = m.astype(BF16).T
            return 0

        lax.fori_loop(0, 16, turn, 0, unroll=4)

    def relayout(h, ds):
        for ab in range(2):
            s = (second(ab) + ds) % 4

            def relay(f, _):
                for k in range(2 * NK):
                    rows = pl.ds(f * 12 + k, 64, stride=49)
                    swap[ab, rows, :] = panel[h, ab, s * 4 + f, k].astype(F32)
                return 0

            lax.fori_loop(0, 4, relay, 0)

            def pack(c, _):
                v = swap[ab, pl.ds(c * 49, 48), :]
                lefts[h, ab * 64 + c, pl.ds(pl.multiple_of(s * 48, 16), 48), :] = v.astype(BF16)
                return 0

            lax.fori_loop(0, 64, pack, 0, unroll=8)

    def multiply(h, p):
        def mul(n, total):
            c2 = p * 16 + n
            for cp in range(2):
                c = (p // 2) * 64 + cp * 32 + (p % 2) * 16 + n
                part = jnp.dot(r_mat[c2, cp * 64 : cp * 64 + 64, :], lefts[h, c], preferred_element_type=F32)
                acc[pl.ds(c * 65, 64), :] = part
                total = total + part
            return total

        start = jnp.zeros((64, 128), F32) if p == 0 else sums[...]
        sums[...] = lax.fori_loop(0, 16, mul, start, unroll=8)

    def finish(h):
        mean = sums[...] * (1.0 / 128)

        def square(c, total):
            centred = acc[pl.ds(c * 65, 64), :] - mean
            return total + centred * centred

        spread = lax.fori_loop(0, 128, square, jnp.zeros((64, 128), F32), unroll=8)
        scale = lax.rsqrt(spread * (1.0 / 128) + 1e-05)

        def normalise(c, _):
            rows = pl.ds(c * 65, 64)
            acc[rows, :] = (acc[rows, :] - mean) * scale * gain_c[pl.ds(c, 1), :] + bias_c[pl.ds(c, 1), :]
            return 0

        lax.fori_loop(0, 128, normalise, 0, unroll=8)

        def columns(b, _):
            turned = [acc[pl.ds(b * 4 + n, 128, stride=65), :].astype(BF16).T for n in range(4)]
            result = jnp.dot(jnp.concatenate(turned, axis=0), wo_ref[...], preferred_element_type=F32)
            for n in range(4):
                proj[pl.ds(b * 4 + n, 128, stride=65), :] = result[n * 128 : n * 128 + 128]
            return 0

        lax.fori_loop(0, 16, columns, 0, unroll=2)

        for part in range(4):
            def body(i, _):
                g = zv[h * 128 + i].astype(F32)
                v = g * proj[pl.ds(i * 65, 64), :]
                zv[h * 128 + i] = v.astype(BF16)
                return 0

            lax.fori_loop(part * 32, part * 32 + 32, body, 0, unroll=8)
            out_copy(h, part).start()

    def out_copy(h, part):
        rows = pl.ds(h * 128 + part * 32, 32)
        return pltpu.make_async_copy(zv.at[rows], out_hbm.at[rows], out_sem.at[h * 4 + part])

    start_r1()
    lax.fori_loop(0, NK, window_left, 0, unroll=3)
    send_z(0)
    send_z(1)
    rest.wait()
    gate_part(0, 4)
    wait_z(0)
    send_p1(0)
    send_q1(0, 0)
    gate_part(4, 8)
    start_r2(0)
    gate_part(8, 12)
    pass_p1(0)
    send_q1(0, -1)
    send_q1(0, 1)
    start_r2(1)
    gate_part(12, 20)
    pass_q1(0, 0)
    wait_p2(0)
    send_q1(0, 2)
    gate_part(20, 28)
    wait_z(1)
    send_p1(1)
    relayout(0, 0)
    gate_part(28, 36)
    pass_q1(0, -1)
    pass_q1(0, 1)
    send_q1(1, 0)
    gate_part(36, 44)
    pass_r2(0)
    gate_part(44, 48)
    pass_q1(0, 2)
    pass_p1(1)
    send_q1(1, -1)
    send_q1(1, 1)
    gate_part(48, 56)
    pass_r2(1)
    gate_part(56, 64)
    relayout(0, -1)
    pass_q1(1, 0)
    wait_p2(1)
    send_q1(1, 2)
    pass_r2(2)
    relayout(0, 1)
    for df in DF:
        wait_q2(0, df)
    relayout(0, 2)
    pass_r2(3)
    pass_q1(1, -1)
    pass_q1(1, 1)
    wait_right(0)
    prep_right(0)
    multiply(0, 0)
    wait_right(1)
    prep_right(1)
    multiply(0, 1)
    relayout(1, 0)
    wait_right(2)
    prep_right(2)
    multiply(0, 2)
    pass_q1(1, 2)
    wait_right(3)
    prep_right(3)
    multiply(0, 3)
    finish(0)
    relayout(1, -1)
    relayout(1, 1)
    for df in DF:
        wait_q2(1, df)
    relayout(1, 2)
    for p in range(4):
        multiply(1, p)
    finish(1)

    for n, c in copies.values():
        c.wait_send()
    for q in range(4):
        @pl.when(jnp.logical_not(r1_mine(q)))
        def _():
            for ab in range(2):
                r1_copy(q, ab).wait_send()

    @pl.when(gathers)
    def _():
        for p in range(4):
            r2_copy(p, 1).wait_send()
            r2_copy(p, 3).wait_send()

        @pl.when(jnp.logical_not(at_home))
        def _():
            for p in range(4):
                r2_copy(p, 0).wait_send()

    @pl.when(relays)
    def _():
        for p in range(4):
            for z in range(2):
                for half in range(2):
                    @pl.when(rel == 1 + 2 * half)
                    def _():
                        far_copy(p, z, half).wait_send()
                r3_copy(p, z).wait_send()

    for h in range(2):
        for part in range(4):
            out_copy(h, part).wait()


def body(*args):
    vmem = pl.BlockSpec(memory_space=pltpu.VMEM)
    anywhere = pl.BlockSpec(memory_space=pl.ANY)
    return pl.pallas_call(
        kernel,
        out_shape=jax.ShapeDtypeStruct((256, 64, 128), BF16),
        in_specs=[anywhere] + [vmem] * 10,
        out_specs=anywhere,
        scratch_shapes=[
            pltpu.VMEM((256, 64, 128), BF16),
            pltpu.VMEM((3104, 128), F32),
            pltpu.VMEM((512, 128), BF16),
            pltpu.VMEM((NK, 256, 128), BF16),
            pltpu.VMEM((2, 2, 16, 12, 64, 128), BF16),
            pltpu.VMEM((4, NK, 64, 128), BF16),
            pltpu.VMEM((16, NK, 64, 128), BF16),
            pltpu.VMEM((2, 16, NK, 64, 128), BF16),
            pltpu.VMEM((64, 128, 192), BF16),
            pltpu.VMEM((2, 128, 192, 128), BF16),
            pltpu.VMEM((2, 64 * 49, 128), F32),
            pltpu.VMEM((128 * 65, 128), F32),
            pltpu.VMEM((64, 128), F32),
            pltpu.VMEM((128 * 65, 128), F32),
            pltpu.VMEM((128, 128), F32),
            pltpu.VMEM((128, 128), F32),
            pltpu.SemaphoreType.DMA((2,)),
            pltpu.SemaphoreType.DMA((8,)),
            pltpu.SemaphoreType.DMA((N_COPIES,)),
            pltpu.SemaphoreType.DMA((N_COPIES,)),
            pltpu.SemaphoreType.DMA((8,)),
            pltpu.SemaphoreType.DMA((2,)),
            pltpu.SemaphoreType.DMA((16,)),
            pltpu.SemaphoreType.DMA((8,)),
            pltpu.SemaphoreType.DMA((8,)),
            pltpu.SemaphoreType.DMA((16,)),
            pltpu.SemaphoreType.DMA((8,)),
            pltpu.SemaphoreType.DMA((8,)),
        ],
        compiler_params=pltpu.CompilerParams(
            collective_id=0, has_side_effects=True, vmem_limit_bytes=60 * 1024 * 1024
        ),
        cost_estimate=pl.CostEstimate(flops=2_000_000_000, bytes_accessed=8_400_000, transcendentals=2_000_000),
    )(*args)


def solution(mesh):
    in_specs = (P("row", "col", None),) + (P(),) * 10
    return jax.shard_map(body, mesh=mesh, in_specs=in_specs, out_specs=P("row", "col", None), check_vma=False)
```

```python
import functools

import jax
import jax.numpy as jnp
from jax import lax
from jax.experimental import pallas as pl
from jax.experimental.pallas import tpu as pltpu
from jax.sharding import PartitionSpec as P

MESH = pl.DeviceIdType.MESH
F32 = jnp.float32
BF16 = jnp.bfloat16
NK = 6
DF = (0, -1, 1, 2)
N_COPIES = 84


def norm_rows(x, gain, bias):
    average = jnp.full((128, 128), 1.0 / 128, BF16)
    centred = x.astype(F32) - jnp.dot(x, average, preferred_element_type=F32)
    spread = jnp.dot((centred * centred).astype(BF16), average, preferred_element_type=F32)
    return (centred * lax.rsqrt(spread + 1e-05) * gain + bias).astype(BF16)


def kernel(
    z_hbm, gin_ref, bin_ref, wlg_ref, wlp_ref, wrg_ref, wrp_ref, wog_ref, gout_ref, bout_ref, wo_ref,
    out_hbm,
    zv, zf, wt, normed_w, panel, r_send, r_gather, r_nat, r_mat, r_last, lefts, swap, acc, sums, proj, gain_c, bias_c,
    z_sem, out_sem, send_sem, recv_sem, r1_send, r1_recv, r2_send, r2_recv, rf_send, rf_recv, r3_send, r3_recv,
):
    row, col = lax.axis_index("row"), lax.axis_index("col")
    zh, core = row // 2, row % 2
    zl, y, x = col // 16, (col // 4) % 4, col % 4

    def dev(zh_=None, core_=None, zl_=None, y_=None, x_=None):
        a = zh if zh_ is None else zh_
        b = core if core_ is None else core_
        c = zl if zl_ is None else zl_
        d = y if y_ is None else y_
        e = x if x_ is None else x_
        return (a * 2 + b, c * 16 + d * 4 + e)

    barrier = pltpu.get_barrier_semaphore()

    def greet(target):
        pl.semaphore_signal(barrier, inc=1, device_id=target, device_id_type=MESH)

    for n in range(1, 16):
        p = (y * 4 + x + n) % 16
        greet(dev(y_=p // 4, x_=p % 4))
    for n in range(1, 8):
        p = (zh * 2 + zl + n) % 8
        greet(dev(zh_=p // 2, zl_=p % 2))
    greet(dev(core_=1 - core))

    head = pltpu.make_async_copy(z_hbm.at[:, pl.ds(0, 16), :], zv.at[:, pl.ds(0, 16), :], z_sem.at[0])
    rest = pltpu.make_async_copy(z_hbm.at[:, pl.ds(16, 48), :], zv.at[:, pl.ds(16, 48), :], z_sem.at[1])
    head.start()
    rest.start()

    gin, bias_in = gin_ref[...].reshape(1, 128), bin_ref[...].reshape(1, 128)
    for n, w in enumerate((wlg_ref, wlp_ref, wrg_ref, wrp_ref)):
        wt[n * 128 : (n + 1) * 128, :] = w[...].astype(F32).T.astype(BF16)
    gain_c[...] = jnp.broadcast_to(gout_ref[...].reshape(1, 128), (128, 128)).T
    bias_c[...] = jnp.broadcast_to(bout_ref[...].reshape(1, 128), (128, 128)).T

    head.wait()

    def widen(b, _):
        i0 = pl.multiple_of(b * 8, 8)
        v = zv[pl.ds(i0, 8), 0:16, :].astype(F32)
        for i in range(8):
            zf[pl.ds((i0 + i) * 9, 8), :] = v[i, 0:8]
        return 0

    lax.fori_loop(0, 32, widen, 0, unroll=4)

    def norm_window(k, _):
        v = zf[pl.ds(k, 256, stride=9), :].astype(BF16)
        normed_w[k] = norm_rows(v, gin, bias_in)
        return 0

    lax.fori_loop(0, NK, norm_window, 0, unroll=3)

    def project(k, part):
        return lax.dot_general(
            wt[part * 256 : part * 256 + 256, :], normed_w[k], (((1,), (1,)), ((), ())), preferred_element_type=F32
        )

    def window_left(k, _):
        both = project(k, 0)
        left = (jax.nn.sigmoid(both[0:128]) * both[128:256]).astype(BF16)
        for h in range(2):
            for ab in range(2):
                pair = (y * 4 + x) if ab == 0 else (x * 4 + y)
                panel[h, ab, pair, zl * NK + k] = left[ab * 64 : ab * 64 + 64, h * 128 : h * 128 + 128]
        return 0

    low = lax.broadcasted_iota(jnp.int32, (32, 128), 1) < 64

    def window_right(k, _):
        both = project(k, 1)
        right = jax.nn.sigmoid(both[0:128]) * both[128:256]
        for u in range(2):
            for ab in range(2):
                lo = right[ab * 64 : ab * 64 + 32, u * 128 : u * 128 + 128]
                hi = right[ab * 64 + 32 : ab * 64 + 64, u * 128 : u * 128 + 128]
                r_send[2 * u, k, ab * 32 : ab * 32 + 32, :] = jnp.where(low, lo, pltpu.roll(hi, 64, 1)).astype(BF16)
                r_send[2 * u + 1, k, ab * 32 : ab * 32 + 32, :] = jnp.where(low, pltpu.roll(lo, 64, 1), hi).astype(BF16)
        return 0

    lax.fori_loop(0, NK, window_right, 0, unroll=3)
    pl.semaphore_wait(barrier, 23)

    count = [0]
    copies = {}

    def left_copy(name, ref, target):
        n = count[0]
        count[0] += 1
        c = pltpu.make_async_remote_copy(
            src_ref=ref, dst_ref=ref, send_sem=send_sem.at[n], recv_sem=recv_sem.at[n], device_id=target, device_id_type=MESH
        )
        c.start()
        copies[name] = (n, c)

    def arrived(name, ref):
        n, _ = copies[name]
        pltpu.make_async_copy(ref, ref, recv_sem.at[n]).wait()

    def first(ab):
        return x if ab == 0 else y

    def second(ab):
        return y if ab == 0 else x

    def step_first(ab, d):
        return dev(x_=(x + d) % 4) if ab == 0 else dev(y_=(y + d) % 4)

    def step_second(ab, d):
        return dev(y_=(y + d) % 4) if ab == 0 else dev(x_=(x + d) % 4)

    def pair_ref(h, ab, ds, df, half=None):
        p = ((second(ab) + ds) % 4) * 4 + (first(ab) + df) % 4
        if half is None:
            return panel.at[h, ab, p]
        return panel.at[h, ab, p, :, pl.ds(half * 32, 32), :]

    def z_ref(h, ab, z):
        return panel.at[h, ab, second(ab) * 4 + first(ab), pl.ds(z * NK, NK)]

    def send_z(h):
        for ab in range(2):
            left_copy(("z", h, ab), z_ref(h, ab, zl), dev(zl_=1 - zl))

    def wait_z(h):
        for ab in range(2):
            arrived(("z", h, ab), z_ref(h, ab, 1 - zl))

    def send_p1(h):
        for ab in range(2):
            for d in (1, -1):
                left_copy(("p1", h, ab, d), pair_ref(h, ab, 0, 0), step_first(ab, d))

    def send_q1(h, df):
        for ab in range(2):
            for d in (1, -1):
                left_copy(("q1", h, ab, df, d), pair_ref(h, ab, 0, df), step_second(ab, d))

    def pass_p1(h):
        for d in (1, -1):
            for ab in range(2):
                arrived(("p1", h, ab, d), pair_ref(h, ab, 0, -d))
                half = 0 if d == 1 else 1
                left_copy(("p2", h, ab, d), pair_ref(h, ab, 0, -d, half), step_first(ab, d))

    def wait_p2(h):
        for d in (1, -1):
            for ab in range(2):
                half = 0 if d == 1 else 1
                arrived(("p2", h, ab, d), pair_ref(h, ab, 0, 2, half))

    def pass_q1(h, df):
        for d in (1, -1):
            for ab in range(2):
                arrived(("q1", h, ab, df, d), pair_ref(h, ab, -d, df))
                half = 0 if d == 1 else 1
                left_copy(("q2", h, ab, df, d), pair_ref(h, ab, -d, df, half), step_second(ab, d))

    def wait_q2(h, df):
        for d in (1, -1):
            for ab in range(2):
                half = 0 if d == 1 else 1
                arrived(("q2", h, ab, df, d), pair_ref(h, ab, 2, df, half))

    own_slot = y * 4 + x
    ty = row % 4
    gathers = jnp.logical_and(y // 2 == zh % 2, core == y % 2)
    relays = core == y % 2

    def r1_ref(ref, n, ab):
        return ref.at[n, :, pl.ds(ab * 32, 32), :]

    def r1_copy(q, ab):
        return pltpu.make_async_remote_copy(
            src_ref=r1_ref(r_send, q, ab), dst_ref=r1_ref(r_gather, own_slot, ab),
            send_sem=r1_send.at[q * 2 + ab], recv_sem=r1_recv.at[ab], device_id=dev(y_=ty, x_=q), device_id_type=MESH,
        )

    def r1_mine(q):
        return jnp.logical_and(ty == y, x == q)

    def start_r1():
        for ab in range(2):
            for q in range(4):
                @pl.when(r1_mine(q))
                def _():
                    pltpu.make_async_copy(r1_ref(r_send, q, ab), r1_ref(r_gather, own_slot, ab), r1_recv.at[ab]).start()

                @pl.when(jnp.logical_not(r1_mine(q)))
                def _():
                    r1_copy(q, ab).start()

    def piece(ref, p):
        return ref.at[:, :, pl.ds(p * 16, 16), :]

    def r2_copy(p, o):
        return pltpu.make_async_remote_copy(
            src_ref=piece(r_gather, p), dst_ref=piece(r_nat.at[zl], p), send_sem=r2_send.at[p * 4 + o],
            recv_sem=r2_recv.at[p * 2 + zl], device_id=dev(zh_=(zh + o) % 4, zl_=zh // 2), device_id_type=MESH,
        )

    at_home = zl == zh // 2

    def start_r2(ab):
        @pl.when(gathers)
        def _():
            got = r_gather.at[:, :, pl.ds(ab * 32, 32), :]
            pltpu.make_async_copy(got, got, r1_recv.at[ab]).wait()
            for p in (2 * ab, 2 * ab + 1):
                r2_copy(p, 1).start()
                r2_copy(p, 3).start()

                @pl.when(at_home)
                def _():
                    pltpu.make_async_copy(piece(r_gather, p), piece(r_nat.at[zl], p), r2_recv.at[p * 2 + zl]).start()

                @pl.when(jnp.logical_not(at_home))
                def _():
                    r2_copy(p, 0).start()

    rel = (zh + 4 - (2 * zl + y // 2)) % 4

    def far_ref(p, z, half):
        return r_nat.at[z, pl.ds(half * 8, 8), :, pl.ds(p * 16, 16), :]

    def far_copy(p, z, half):
        return pltpu.make_async_remote_copy(
            src_ref=far_ref(p, z, half), dst_ref=far_ref(p, z, half), send_sem=rf_send.at[p * 2 + z],
            recv_sem=rf_recv.at[p * 4 + z * 2 + half],
            device_id=dev(zh_=(zh + (1 if half == 0 else 3)) % 4), device_id_type=MESH,
        )

    def r3_copy(p, z):
        part = piece(r_nat.at[z], p)
        return pltpu.make_async_remote_copy(
            src_ref=part, dst_ref=part, send_sem=r3_send.at[p * 2 + z], recv_sem=r3_recv.at[p * 2 + z],
            device_id=dev(core_=1 - core), device_id_type=MESH,
        )

    def pass_r2(p):
        @pl.when(jnp.logical_and(relays, rel != 2))
        def _():
            for z in range(2):
                part = piece(r_nat.at[z], p)
                pltpu.make_async_copy(part, part, r2_recv.at[p * 2 + z]).wait()
                for half in range(2):
                    @pl.when(rel == 1 + 2 * half)
                    def _():
                        far_copy(p, z, half).start()
                r3_copy(p, z).start()

    def wait_right(p):
        @pl.when(jnp.logical_and(relays, rel == 2))
        def _():
            for z in range(2):
                for half in range(2):
                    part = far_ref(p, z, half)
                    pltpu.make_async_copy(part, part, rf_recv.at[p * 4 + z * 2 + half]).wait()
                r3_copy(p, z).start()

        @pl.when(jnp.logical_not(relays))
        def _():
            for z in range(2):
                part = piece(r_nat.at[z], p)
                pltpu.make_async_copy(part, part, r3_recv.at[p * 2 + z]).wait()

    def gate_part(lo, hi):
        def body(b, _):
            i0 = pl.multiple_of(b * 16, 16)
            normed = norm_rows(zv[pl.ds(i0, 16)].reshape(1024, 128), gin, bias_in)
            g = jax.nn.sigmoid(jnp.dot(normed, wog_ref[...], preferred_element_type=F32))
            zv[pl.ds(i0, 16)] = g.astype(BF16).reshape(16, 64, 128)
            return 0

        lax.fori_loop(lo // 4, hi // 4, body, 0)

    def prep_right(p):
        ab = p // 2

        def relay(d, _):
            s = (second(ab) + d + 3) % 4
            for f in range(4):
                slot_ = (s * 4 + f) if ab == 0 else (f * 4 + s)
                for z in range(2):
                    for k in range(NK):
                        zf[pl.ds(d * 48 + f * 12 + z * NK + k, 16, stride=193), :] = r_nat[
                            z, slot_, k, p * 16 : p * 16 + 16, :
                        ].astype(F32)
            return 0

        lax.fori_loop(0, 4, relay, 0)

        def turn(c, _):
            r_mat[p * 16 + c] = zf[pl.ds(c * 193, 192), :].astype(BF16).T
            r_last[p * 16 + c] = zf[pl.ds(c * 193 + 144, 48), :].astype(BF16).T
            return 0

        lax.fori_loop(0, 16, turn, 0, unroll=4)

    def spread_rows(h, ab, ds):
        s = (second(ab) + ds) % 4

        def relay(f, _):
            for k in range(2 * NK):
                rows = pl.ds(f * 12 + k, 64, stride=49)
                swap[ab, rows, :] = panel[h, ab, s * 4 + f, k].astype(F32)
            return 0

        lax.fori_loop(0, 4, relay, 0)

    def relayout(h, ds):
        for ab in range(2):
            spread_rows(h, ab, ds)

            def pack(c, _):
                v = swap[ab, pl.ds(c * 49, 48), :]
                lefts[h, ab * 64 + c, (ds + 1) * 48 : (ds + 2) * 48, :] = v.astype(BF16)
                return 0

            lax.fori_loop(0, 64, pack, 0, unroll=8)

    def multiply(h, p, depth):
        def mul(n, total):
            c2 = p * 16 + n
            for cp in range(2):
                c = (p // 2) * 64 + cp * 32 + (p % 2) * 16 + n
                right = r_mat[c2, cp * 64 : cp * 64 + 64, 0:depth]
                part = jnp.dot(right, lefts[h, c, 0:depth, :], preferred_element_type=F32)
                acc[pl.ds(c * 65, 64), :] = part
                total = total + part
            return total

        start = jnp.zeros((64, 128), F32) if p == 0 else sums[...]
        sums[...] = lax.fori_loop(0, 16, mul, start, unroll=8)

    def add_last(h):
        for ab in range(2):
            spread_rows(h, ab, 2)

            def mul(c2, total):
                for cp in range(2):
                    c = cp * 32 + c2
                    left = swap[ab, pl.ds(c * 49, 48), :].astype(BF16)
                    right = r_last[ab * 32 + c2, cp * 64 : cp * 64 + 64, :]
                    part = jnp.dot(right, left, preferred_element_type=F32)
                    acc[pl.ds((ab * 64 + c) * 65, 64), :] += part
                    total = total + part
                return total

            sums[...] = lax.fori_loop(0, 32, mul, sums[...], unroll=8)

    def finish(h):
        mean = sums[...] * (1.0 / 128)

        def square(c, total):
            centred = acc[pl.ds(c * 65, 64), :] - mean
            return total + centred * centred

        spread = lax.fori_loop(0, 128, square, jnp.zeros((64, 128), F32), unroll=8)
        scale = lax.rsqrt(spread * (1.0 / 128) + 1e-05)

        def normalise(c, _):
            rows = pl.ds(c * 65, 64)
            acc[rows, :] = (acc[rows, :] - mean) * scale * gain_c[pl.ds(c, 1), :] + bias_c[pl.ds(c, 1), :]
            return 0

        lax.fori_loop(0, 128, normalise, 0, unroll=8)

        def columns(b, _):
            turned = [acc[pl.ds(b * 4 + n, 128, stride=65), :].astype(BF16).T for n in range(4)]
            result = jnp.dot(jnp.concatenate(turned, axis=0), wo_ref[...], preferred_element_type=F32)
            for n in range(4):
                proj[pl.ds(b * 4 + n, 128, stride=65), :] = result[n * 128 : n * 128 + 128]
            return 0

        lax.fori_loop(0, 16, columns, 0, unroll=2)

        for part in range(4):
            def body(i, _):
                g = zv[h * 128 + i].astype(F32)
                v = g * proj[pl.ds(i * 65, 64), :]
                zv[h * 128 + i] = v.astype(BF16)
                return 0

            lax.fori_loop(part * 32, part * 32 + 32, body, 0, unroll=8)
            out_copy(h, part).start()

    def out_copy(h, part):
        rows = pl.ds(h * 128 + part * 32, 32)
        return pltpu.make_async_copy(zv.at[rows], out_hbm.at[rows], out_sem.at[h * 4 + part])

    start_r1()
    lax.fori_loop(0, NK, window_left, 0, unroll=3)
    send_z(0)
    send_z(1)
    rest.wait()
    gate_part(0, 4)
    wait_z(0)
    send_p1(0)
    send_q1(0, 0)
    gate_part(4, 8)
    start_r2(0)
    gate_part(8, 12)
    pass_p1(0)
    send_q1(0, -1)
    send_q1(0, 1)
    start_r2(1)
    gate_part(12, 20)
    pass_q1(0, 0)
    wait_p2(0)
    send_q1(0, 2)
    gate_part(20, 28)
    wait_z(1)
    send_p1(1)
    relayout(0, 0)
    gate_part(28, 36)
    pass_q1(0, -1)
    pass_q1(0, 1)
    send_q1(1, 0)
    gate_part(36, 44)
    pass_r2(0)
    gate_part(44, 48)
    pass_q1(0, 2)
    pass_p1(1)
    send_q1(1, -1)
    send_q1(1, 1)
    gate_part(48, 56)
    pass_r2(1)
    gate_part(56, 64)
    relayout(0, -1)
    pass_q1(1, 0)
    wait_p2(1)
    send_q1(1, 2)
    pass_r2(2)
    relayout(0, 1)
    for df in DF:
        wait_q2(0, df)
    relayout(0, 2)
    pass_r2(3)
    pass_q1(1, -1)
    pass_q1(1, 1)
    wait_right(0)
    prep_right(0)
    multiply(0, 0, 192)
    wait_right(1)
    prep_right(1)
    multiply(0, 1, 192)
    relayout(1, 0)
    wait_right(2)
    prep_right(2)
    multiply(0, 2, 192)
    pass_q1(1, 2)
    relayout(1, -1)
    relayout(1, 1)
    wait_right(3)
    prep_right(3)
    multiply(0, 3, 192)
    finish(0)
    for p in range(4):
        multiply(1, p, 144)
    for df in DF:
        wait_q2(1, df)
    add_last(1)
    finish(1)

    for n, c in copies.values():
        c.wait_send()
    for q in range(4):
        @pl.when(jnp.logical_not(r1_mine(q)))
        def _():
            for ab in range(2):
                r1_copy(q, ab).wait_send()

    @pl.when(gathers)
    def _():
        for p in range(4):
            r2_copy(p, 1).wait_send()
            r2_copy(p, 3).wait_send()

        @pl.when(jnp.logical_not(at_home))
        def _():
            for p in range(4):
                r2_copy(p, 0).wait_send()

    @pl.when(relays)
    def _():
        for p in range(4):
            for z in range(2):
                for half in range(2):
                    @pl.when(rel == 1 + 2 * half)
                    def _():
                        far_copy(p, z, half).wait_send()
                r3_copy(p, z).wait_send()

    for h in range(2):
        for part in range(4):
            out_copy(h, part).wait()


def copy_kernel(x_ref, o_ref):
    o_ref[...] = x_ref[...]


def body(*args):
    vmem = pl.BlockSpec(memory_space=pltpu.VMEM)
    anywhere = pl.BlockSpec(memory_space=pl.ANY)
    update = pl.pallas_call(
        kernel,
        out_shape=jax.ShapeDtypeStruct((256, 64, 128), BF16),
        in_specs=[anywhere] + [vmem] * 10,
        out_specs=anywhere,
        scratch_shapes=[
            pltpu.VMEM((256, 64, 128), BF16),
            pltpu.VMEM((3104, 128), F32),
            pltpu.VMEM((512, 128), BF16),
            pltpu.VMEM((NK, 256, 128), BF16),
            pltpu.VMEM((2, 2, 16, 12, 64, 128), BF16),
            pltpu.VMEM((4, NK, 64, 128), BF16),
            pltpu.VMEM((16, NK, 64, 128), BF16),
            pltpu.VMEM((2, 16, NK, 64, 128), BF16),
            pltpu.VMEM((64, 128, 192), BF16),
            pltpu.VMEM((64, 128, 48), BF16),
            pltpu.VMEM((2, 128, 192, 128), BF16),
            pltpu.VMEM((2, 64 * 49, 128), F32),
            pltpu.VMEM((128 * 65, 128), F32),
            pltpu.VMEM((64, 128), F32),
            pltpu.VMEM((128 * 65, 128), F32),
            pltpu.VMEM((128, 128), F32),
            pltpu.VMEM((128, 128), F32),
            pltpu.SemaphoreType.DMA((2,)),
            pltpu.SemaphoreType.DMA((8,)),
            pltpu.SemaphoreType.DMA((N_COPIES,)),
            pltpu.SemaphoreType.DMA((N_COPIES,)),
            pltpu.SemaphoreType.DMA((8,)),
            pltpu.SemaphoreType.DMA((2,)),
            pltpu.SemaphoreType.DMA((16,)),
            pltpu.SemaphoreType.DMA((8,)),
            pltpu.SemaphoreType.DMA((8,)),
            pltpu.SemaphoreType.DMA((16,)),
            pltpu.SemaphoreType.DMA((8,)),
            pltpu.SemaphoreType.DMA((8,)),
        ],
        compiler_params=pltpu.CompilerParams(
            collective_id=0, has_side_effects=True, vmem_limit_bytes=60 * 1024 * 1024
        ),
        cost_estimate=pl.CostEstimate(flops=2_000_000_000, bytes_accessed=8_400_000, transcendentals=2_000_000),
    )(*args)
    block = pl.BlockSpec((32, 64, 128), lambda i: (i, 0, 0))
    return pl.pallas_call(
        copy_kernel,
        out_shape=jax.ShapeDtypeStruct((256, 64, 128), BF16),
        grid=(8,),
        in_specs=[block],
        out_specs=block,
        compiler_params=pltpu.CompilerParams(vmem_limit_bytes=60 * 1024 * 1024),
        cost_estimate=pl.CostEstimate(flops=0, bytes_accessed=8_400_000, transcendentals=0),
    )(update)


def solution(mesh):
    in_specs = (P("row", "col", None),) + (P(),) * 10
    return jax.shard_map(body, mesh=mesh, in_specs=in_specs, out_specs=P("row", "col", None), check_vma=False)
```

```python
from functools import partial

import jax
import jax.numpy as jnp
from jax import lax
from jax.experimental import pallas as pl
from jax.experimental.pallas import tpu as pltpu
from jax.sharding import PartitionSpec as P

MESH = pl.DeviceIdType.MESH
F32 = jnp.float32
BF16 = jnp.bfloat16
NK = 6
DF = (0, -1, 1, 2)
N_COPIES = 84


def norm_rows(x, gain, bias):
    average = jnp.full((128, 128), 1.0 / 128, BF16)
    centred = x.astype(F32) - jnp.dot(x, average, preferred_element_type=F32)
    spread = jnp.dot((centred * centred).astype(BF16), average, preferred_element_type=F32)
    return (centred * lax.rsqrt(spread + 1e-05) * gain + bias).astype(BF16)


def kernel(
    z_hbm, gin_ref, bin_ref, wlg_ref, wlp_ref, wrg_ref, wrp_ref, wog_ref, gout_ref, bout_ref, wo_ref,
    out_hbm,
    zv, zf, wt, normed_w, panel, r_send, r_gather, r_nat, r_mat, lefts, swap, acc, sums, proj, gain_c, bias_c,
    z_sem, out_sem, send_sem, recv_sem, r1_send, r1_recv, r2_send, r2_recv, rf_send, rf_recv, r3_send, r3_recv,
):
    row, col = lax.axis_index("row"), lax.axis_index("col")
    zh, core = row // 2, row % 2
    zl, y, x = col // 16, (col // 4) % 4, col % 4

    def dev(zh_=None, core_=None, zl_=None, y_=None, x_=None):
        a = zh if zh_ is None else zh_
        b = core if core_ is None else core_
        c = zl if zl_ is None else zl_
        d = y if y_ is None else y_
        e = x if x_ is None else x_
        return (a * 2 + b, c * 16 + d * 4 + e)

    barrier = pltpu.get_barrier_semaphore()

    def greet(target):
        pl.semaphore_signal(barrier, inc=1, device_id=target, device_id_type=MESH)

    for n in range(1, 16):
        p = (y * 4 + x + n) % 16
        greet(dev(y_=p // 4, x_=p % 4))
    for n in range(1, 8):
        p = (zh * 2 + zl + n) % 8
        greet(dev(zh_=p // 2, zl_=p % 2))
    greet(dev(core_=1 - core))

    head = pltpu.make_async_copy(z_hbm.at[:, pl.ds(0, 16), :], zv.at[:, pl.ds(0, 16), :], z_sem.at[0])
    rest = pltpu.make_async_copy(z_hbm.at[:, pl.ds(16, 48), :], zv.at[:, pl.ds(16, 48), :], z_sem.at[1])
    head.start()
    rest.start()

    gin, bias_in = gin_ref[...].reshape(1, 128), bin_ref[...].reshape(1, 128)
    for n, w in enumerate((wlg_ref, wlp_ref, wrg_ref, wrp_ref)):
        wt[n * 128 : (n + 1) * 128, :] = w[...].astype(F32).T.astype(BF16)
    gain_c[...] = jnp.broadcast_to(gout_ref[...].reshape(1, 128), (128, 128)).T
    bias_c[...] = jnp.broadcast_to(bout_ref[...].reshape(1, 128), (128, 128)).T

    head.wait()

    def widen(b, _):
        i0 = pl.multiple_of(b * 8, 8)
        v = zv[pl.ds(i0, 8), 0:16, :].astype(F32)
        for i in range(8):
            zf[pl.ds((i0 + i) * 9, 8), :] = v[i, 0:8]
        return 0

    lax.fori_loop(0, 32, widen, 0, unroll=4)

    def norm_window(k, _):
        v = zf[pl.ds(k, 256, stride=9), :].astype(BF16)
        normed_w[k] = norm_rows(v, gin, bias_in)
        return 0

    lax.fori_loop(0, NK, norm_window, 0, unroll=3)

    def project(k, part):
        return lax.dot_general(
            wt[part * 256 : part * 256 + 256, :], normed_w[k], (((1,), (1,)), ((), ())), preferred_element_type=F32
        )

    def window_left(k, _):
        both = project(k, 0)
        left = (jax.nn.sigmoid(both[0:128]) * both[128:256]).astype(BF16)
        for h in range(2):
            for ab in range(2):
                pair = (y * 4 + x) if ab == 0 else (x * 4 + y)
                panel[h, ab, pair, zl * NK + k] = left[ab * 64 : ab * 64 + 64, h * 128 : h * 128 + 128]
        return 0

    low = lax.broadcasted_iota(jnp.int32, (32, 128), 1) < 64

    def window_right(k, _):
        both = project(k, 1)
        right = jax.nn.sigmoid(both[0:128]) * both[128:256]
        for u in range(2):
            for ab in range(2):
                lo = right[ab * 64 : ab * 64 + 32, u * 128 : u * 128 + 128]
                hi = right[ab * 64 + 32 : ab * 64 + 64, u * 128 : u * 128 + 128]
                r_send[2 * u, k, ab * 32 : ab * 32 + 32, :] = jnp.where(low, lo, pltpu.roll(hi, 64, 1)).astype(BF16)
                r_send[2 * u + 1, k, ab * 32 : ab * 32 + 32, :] = jnp.where(low, pltpu.roll(lo, 64, 1), hi).astype(BF16)
        return 0

    lax.fori_loop(0, NK, window_right, 0, unroll=3)
    pl.semaphore_wait(barrier, 23)

    copies = {}

    def left_copy(name, ref, target):
        if name not in copies:
            copies[name] = len(copies), ref, target
        left_made(name).start()

    def left_made(name):
        n, ref, target = copies[name]
        return pltpu.make_async_remote_copy(
            src_ref=ref(), dst_ref=ref(), send_sem=send_sem.at[n], recv_sem=recv_sem.at[n], device_id=target(),
            device_id_type=MESH,
        )

    def arrived(name, ref):
        n = copies[name][0]
        pltpu.make_async_copy(ref, ref, recv_sem.at[n]).wait()

    def first(ab):
        return x if ab == 0 else y

    def second(ab):
        return y if ab == 0 else x

    def step_first(ab, d):
        return dev(x_=(x + d) % 4) if ab == 0 else dev(y_=(y + d) % 4)

    def step_second(ab, d):
        return dev(y_=(y + d) % 4) if ab == 0 else dev(x_=(x + d) % 4)

    def pair_ref(h, ab, ds, df, half=None):
        p = ((second(ab) + ds) % 4) * 4 + (first(ab) + df) % 4
        if half is None:
            return panel.at[h, ab, p]
        return panel.at[h, ab, p, :, pl.ds(half * 32, 32), :]

    def z_ref(h, ab, z):
        return panel.at[h, ab, second(ab) * 4 + first(ab), pl.ds(z * NK, NK)]

    def send_z(h):
        for ab in range(2):
            left_copy(("z", h, ab), partial(z_ref, h, ab, zl), partial(dev, zl_=1 - zl))

    def wait_z(h):
        for ab in range(2):
            arrived(("z", h, ab), z_ref(h, ab, 1 - zl))

    def send_p1(h):
        for ab in range(2):
            for d in (1, -1):
                left_copy(("p1", h, ab, d), partial(pair_ref, h, ab, 0, 0), partial(step_first, ab, d))

    def send_q1(h, df):
        for ab in range(2):
            for d in (1, -1):
                left_copy(("q1", h, ab, df, d), partial(pair_ref, h, ab, 0, df), partial(step_second, ab, d))

    def pass_p1(h):
        for d in (1, -1):
            for ab in range(2):
                arrived(("p1", h, ab, d), pair_ref(h, ab, 0, -d))
                half = 0 if d == 1 else 1
                left_copy(("p2", h, ab, d), partial(pair_ref, h, ab, 0, -d, half), partial(step_first, ab, d))

    def wait_p2(h):
        for d in (1, -1):
            for ab in range(2):
                half = 0 if d == 1 else 1
                arrived(("p2", h, ab, d), pair_ref(h, ab, 0, 2, half))

    def pass_q1(h, df):
        for d in (1, -1):
            for ab in range(2):
                arrived(("q1", h, ab, df, d), pair_ref(h, ab, -d, df))
                half = 0 if d == 1 else 1
                left_copy(("q2", h, ab, df, d), partial(pair_ref, h, ab, -d, df, half), partial(step_second, ab, d))

    def wait_q2(h, df):
        for d in (1, -1):
            for ab in range(2):
                half = 0 if d == 1 else 1
                arrived(("q2", h, ab, df, d), pair_ref(h, ab, 2, df, half))

    own_slot = y * 4 + x
    ty = row % 4
    gathers = jnp.logical_and(y // 2 == zh % 2, core == y % 2)
    relays = core == y % 2

    def r1_ref(ref, n, ab):
        return ref.at[n, :, pl.ds(ab * 32, 32), :]

    def r1_copy(q, ab):
        return pltpu.make_async_remote_copy(
            src_ref=r1_ref(r_send, q, ab), dst_ref=r1_ref(r_gather, own_slot, ab),
            send_sem=r1_send.at[q * 2 + ab], recv_sem=r1_recv.at[ab], device_id=dev(y_=ty, x_=q), device_id_type=MESH,
        )

    def r1_mine(q):
        return jnp.logical_and(ty == y, x == q)

    def start_r1():
        for ab in range(2):
            for q in range(4):
                @pl.when(r1_mine(q))
                def _():
                    pltpu.make_async_copy(r1_ref(r_send, q, ab), r1_ref(r_gather, own_slot, ab), r1_recv.at[ab]).start()

                @pl.when(jnp.logical_not(r1_mine(q)))
                def _():
                    r1_copy(q, ab).start()

    def piece(ref, p):
        return ref.at[:, :, pl.ds(p * 16, 16), :]

    def r2_copy(p, o):
        return pltpu.make_async_remote_copy(
            src_ref=piece(r_gather, p), dst_ref=piece(r_nat.at[zl], p), send_sem=r2_send.at[p * 4 + o],
            recv_sem=r2_recv.at[p * 2 + zl], device_id=dev(zh_=(zh + o) % 4, zl_=zh // 2), device_id_type=MESH,
        )

    at_home = zl == zh // 2

    def start_r2(ab):
        @pl.when(gathers)
        def _():
            got = r_gather.at[:, :, pl.ds(ab * 32, 32), :]
            pltpu.make_async_copy(got, got, r1_recv.at[ab]).wait()
            for p in (2 * ab, 2 * ab + 1):
                r2_copy(p, 1).start()
                r2_copy(p, 3).start()

                @pl.when(at_home)
                def _():
                    pltpu.make_async_copy(piece(r_gather, p), piece(r_nat.at[zl], p), r2_recv.at[p * 2 + zl]).start()

                @pl.when(jnp.logical_not(at_home))
                def _():
                    r2_copy(p, 0).start()

    rel = (zh + 4 - (2 * zl + y // 2)) % 4

    def far_ref(p, z, half):
        return r_nat.at[z, pl.ds(half * 8, 8), :, pl.ds(p * 16, 16), :]

    def far_copy(p, z, half):
        return pltpu.make_async_remote_copy(
            src_ref=far_ref(p, z, half), dst_ref=far_ref(p, z, half), send_sem=rf_send.at[p * 2 + z],
            recv_sem=rf_recv.at[p * 4 + z * 2 + half],
            device_id=dev(zh_=(zh + (1 if half == 0 else 3)) % 4), device_id_type=MESH,
        )

    def r3_copy(p, z):
        part = piece(r_nat.at[z], p)
        return pltpu.make_async_remote_copy(
            src_ref=part, dst_ref=part, send_sem=r3_send.at[p * 2 + z], recv_sem=r3_recv.at[p * 2 + z],
            device_id=dev(core_=1 - core), device_id_type=MESH,
        )

    def pass_r2(p):
        @pl.when(jnp.logical_and(relays, rel != 2))
        def _():
            for z in range(2):
                part = piece(r_nat.at[z], p)
                pltpu.make_async_copy(part, part, r2_recv.at[p * 2 + z]).wait()
                for half in range(2):
                    @pl.when(rel == 1 + 2 * half)
                    def _():
                        far_copy(p, z, half).start()
                r3_copy(p, z).start()

    def wait_right(p):
        @pl.when(jnp.logical_and(relays, rel == 2))
        def _():
            for z in range(2):
                for half in range(2):
                    part = far_ref(p, z, half)
                    pltpu.make_async_copy(part, part, rf_recv.at[p * 4 + z * 2 + half]).wait()
                r3_copy(p, z).start()

        @pl.when(jnp.logical_not(relays))
        def _():
            for z in range(2):
                part = piece(r_nat.at[z], p)
                pltpu.make_async_copy(part, part, r3_recv.at[p * 2 + z]).wait()

    def gate_part(lo, hi):
        def body(b, _):
            i0 = pl.multiple_of(b * 16, 16)
            normed = norm_rows(zv[pl.ds(i0, 16)].reshape(1024, 128), gin, bias_in)
            g = jax.nn.sigmoid(jnp.dot(normed, wog_ref[...], preferred_element_type=F32))
            zv[pl.ds(i0, 16)] = g.astype(BF16).reshape(16, 64, 128)
            return 0

        lax.fori_loop(lo // 4, hi // 4, body, 0)

    def prep_right(p):
        ab = p // 2

        def relay(s, _):
            for f in range(4):
                slot_ = (s * 4 + f) if ab == 0 else (f * 4 + s)
                for z in range(2):
                    for k in range(NK):
                        zf[pl.ds(s * 48 + f * 12 + z * NK + k, 16, stride=193), :] = r_nat[
                            z, slot_, k, p * 16 : p * 16 + 16, :
                        ].astype(F32)
            return 0

        lax.fori_loop(0, 4, relay, 0)

        def turn(c, _):
            m = zf[pl.ds(c * 193, 192), :]
            r_mat[p * 16 + c] = m.astype(BF16).T
            return 0

        lax.fori_loop(0, 16, turn, 0, unroll=4)

    def relayout(h, ds):
        for ab in range(2):
            s = (second(ab) + ds) % 4

            def relay(f, _):
                for k in range(2 * NK):
                    rows = pl.ds(f * 12 + k, 64, stride=49)
                    swap[ab, rows, :] = panel[h, ab, s * 4 + f, k].astype(F32)
                return 0

            lax.fori_loop(0, 4, relay, 0)

            def pack(c, _):
                v = swap[ab, pl.ds(c * 49, 48), :]
                lefts[h, ab * 64 + c, pl.ds(pl.multiple_of(s * 48, 16), 48), :] = v.astype(BF16)
                return 0

            lax.fori_loop(0, 64, pack, 0, unroll=8)

    def multiply(h, p):
        def mul(n, total):
            c2 = p * 16 + n
            for cp in range(2):
                c = (p // 2) * 64 + cp * 32 + (p % 2) * 16 + n
                part = jnp.dot(r_mat[c2, cp * 64 : cp * 64 + 64, :], lefts[h, c], preferred_element_type=F32)
                acc[pl.ds(c * 65, 64), :] = part
                total = total + part
            return total

        start = jnp.zeros((64, 128), F32) if p == 0 else sums[...]
        sums[...] = lax.fori_loop(0, 16, mul, start, unroll=8)

    def normalise_product():
        mean = sums[...] * (1.0 / 128)

        def square(c, total):
            centred = acc[pl.ds(c * 65, 64), :] - mean
            return total + centred * centred

        spread = lax.fori_loop(0, 128, square, jnp.zeros((64, 128), F32), unroll=8)
        scale = lax.rsqrt(spread * (1.0 / 128) + 1e-05)

        def normalise(c, _):
            rows = pl.ds(c * 65, 64)
            acc[rows, :] = (acc[rows, :] - mean) * scale * gain_c[pl.ds(c, 1), :] + bias_c[pl.ds(c, 1), :]
            return 0

        lax.fori_loop(0, 128, normalise, 0, unroll=8)

    def finish(h):
        def columns(b, _):
            turned = [acc[pl.ds(b * 4 + n, 128, stride=65), :].astype(BF16).T for n in range(4)]
            result = jnp.dot(jnp.concatenate(turned, axis=0), wo_ref[...], preferred_element_type=F32)
            for n in range(4):
                proj[pl.ds(b * 4 + n, 128, stride=65), :] = result[n * 128 : n * 128 + 128]
            return 0

        lax.fori_loop(0, 16, columns, 0, unroll=2)

        for part in range(4):
            def body(i, _):
                g = zv[h * 128 + i].astype(F32)
                v = g * proj[pl.ds(i * 65, 64), :]
                zv[h * 128 + i] = v.astype(BF16)
                return 0

            lax.fori_loop(part * 32, part * 32 + 32, body, 0, unroll=8)
            out_copy(h, part).start()

    def out_copy(h, part):
        rows = pl.ds(h * 128 + part * 32, 32)
        return pltpu.make_async_copy(zv.at[rows], out_hbm.at[rows], out_sem.at[h * 4 + part])

    start_r1()
    lax.fori_loop(0, NK, window_left, 0, unroll=3)
    send_z(0)
    send_z(1)
    rest.wait()
    gate_part(0, 4)
    wait_z(0)
    send_p1(0)
    send_q1(0, 0)
    gate_part(4, 8)
    start_r2(0)
    gate_part(8, 12)
    pass_p1(0)
    send_q1(0, -1)
    send_q1(0, 1)
    start_r2(1)
    gate_part(12, 20)
    pass_q1(0, 0)
    wait_p2(0)
    send_q1(0, 2)
    gate_part(20, 28)
    wait_z(1)
    send_p1(1)
    relayout(0, 0)
    gate_part(28, 36)
    pass_q1(0, -1)
    pass_q1(0, 1)
    send_q1(1, 0)
    gate_part(36, 44)
    pass_r2(0)
    gate_part(44, 48)
    pass_q1(0, 2)
    pass_p1(1)
    send_q1(1, -1)
    send_q1(1, 1)
    gate_part(48, 56)
    pass_r2(1)
    gate_part(56, 64)
    relayout(0, -1)
    pass_q1(1, 0)
    wait_p2(1)
    send_q1(1, 2)
    pass_r2(2)
    relayout(0, 1)
    for df in DF:
        wait_q2(0, df)
    relayout(0, 2)
    pass_r2(3)
    pass_q1(1, -1)
    pass_q1(1, 1)
    for p in range(2):
        wait_right(p)
        prep_right(p)
        multiply(0, p)
    relayout(1, 0)
    wait_right(2)
    prep_right(2)
    multiply(0, 2)

    @pl.when(rel == 2)
    def _():
        pass_q1(1, 2)

    wait_right(3)
    prep_right(3)
    multiply(0, 3)
    normalise_product()

    @pl.when(rel != 2)
    def _():
        pass_q1(1, 2)

    finish(0)
    relayout(1, -1)
    relayout(1, 1)
    for df in DF:
        wait_q2(1, df)
    relayout(1, 2)
    for p in range(4):
        multiply(1, p)
    normalise_product()
    finish(1)

    for name in copies:
        left_made(name).wait_send()
    for q in range(4):
        @pl.when(jnp.logical_not(r1_mine(q)))
        def _():
            for ab in range(2):
                r1_copy(q, ab).wait_send()

    @pl.when(gathers)
    def _():
        for p in range(4):
            r2_copy(p, 1).wait_send()
            r2_copy(p, 3).wait_send()

        @pl.when(jnp.logical_not(at_home))
        def _():
            for p in range(4):
                r2_copy(p, 0).wait_send()

    @pl.when(relays)
    def _():
        for p in range(4):
            for z in range(2):
                for half in range(2):
                    @pl.when(rel == 1 + 2 * half)
                    def _():
                        far_copy(p, z, half).wait_send()
                r3_copy(p, z).wait_send()

    for h in range(2):
        for part in range(4):
            out_copy(h, part).wait()


def body(*args):
    vmem = pl.BlockSpec(memory_space=pltpu.VMEM)
    anywhere = pl.BlockSpec(memory_space=pl.ANY)
    return pl.pallas_call(
        kernel,
        out_shape=jax.ShapeDtypeStruct((256, 64, 128), BF16),
        in_specs=[anywhere] + [vmem] * 10,
        out_specs=anywhere,
        scratch_shapes=[
            pltpu.VMEM((256, 64, 128), BF16),
            pltpu.VMEM((3104, 128), F32),
            pltpu.VMEM((512, 128), BF16),
            pltpu.VMEM((NK, 256, 128), BF16),
            pltpu.VMEM((2, 2, 16, 12, 64, 128), BF16),
            pltpu.VMEM((4, NK, 64, 128), BF16),
            pltpu.VMEM((16, NK, 64, 128), BF16),
            pltpu.VMEM((2, 16, NK, 64, 128), BF16),
            pltpu.VMEM((64, 128, 192), BF16),
            pltpu.VMEM((2, 128, 192, 128), BF16),
            pltpu.VMEM((2, 64 * 49, 128), F32),
            pltpu.VMEM((128 * 65, 128), F32),
            pltpu.VMEM((64, 128), F32),
            pltpu.VMEM((128 * 65, 128), F32),
            pltpu.VMEM((128, 128), F32),
            pltpu.VMEM((128, 128), F32),
            pltpu.SemaphoreType.DMA((2,)),
            pltpu.SemaphoreType.DMA((8,)),
            pltpu.SemaphoreType.DMA((N_COPIES,)),
            pltpu.SemaphoreType.DMA((N_COPIES,)),
            pltpu.SemaphoreType.DMA((8,)),
            pltpu.SemaphoreType.DMA((2,)),
            pltpu.SemaphoreType.DMA((16,)),
            pltpu.SemaphoreType.DMA((8,)),
            pltpu.SemaphoreType.DMA((8,)),
            pltpu.SemaphoreType.DMA((16,)),
            pltpu.SemaphoreType.DMA((8,)),
            pltpu.SemaphoreType.DMA((8,)),
        ],
        compiler_params=pltpu.CompilerParams(
            collective_id=0, has_side_effects=True, vmem_limit_bytes=60 * 1024 * 1024
        ),
        cost_estimate=pl.CostEstimate(flops=2_000_000_000, bytes_accessed=8_400_000, transcendentals=2_000_000),
    )(*args)


def solution(mesh):
    in_specs = (P("row", "col", None),) + (P(),) * 10
    return jax.shard_map(body, mesh=mesh, in_specs=in_specs, out_specs=P("row", "col", None), check_vma=False)
```

```python
from functools import partial

import jax
import jax.numpy as jnp
from jax import lax
from jax.experimental import pallas as pl
from jax.experimental.pallas import tpu as pltpu
from jax.sharding import PartitionSpec as P

MESH = pl.DeviceIdType.MESH
F32 = jnp.float32
BF16 = jnp.bfloat16
NK = 6
DF = (0, -1, 1, 2)
N_COPIES = 84


def norm_rows(x, gain, bias):
    average = jnp.full((128, 128), 1.0 / 128, BF16)
    centred = x.astype(F32) - jnp.dot(x, average, preferred_element_type=F32)
    spread = jnp.dot((centred * centred).astype(BF16), average, preferred_element_type=F32)
    return (centred * lax.rsqrt(spread + 1e-05) * gain + bias).astype(BF16)


def kernel(
    z_hbm, gin_ref, bin_ref, wlg_ref, wlp_ref, wrg_ref, wrp_ref, wog_ref, gout_ref, bout_ref, wo_ref,
    out_hbm,
    zv, zf, wt, normed_w, panel, r_send, r_gather, r_nat, r_mat, lefts, swap, acc, sums, proj, gain_c, bias_c,
    z_sem, out_sem, send_sem, recv_sem, r1_send, r1_recv, r2_send, r2_recv, rf_send, rf_recv, r3_send, r3_recv,
):
    row, col = lax.axis_index("row"), lax.axis_index("col")
    zh, core = row // 2, row % 2
    zl, y, x = col // 16, (col // 4) % 4, col % 4

    def dev(zh_=None, core_=None, zl_=None, y_=None, x_=None):
        a = zh if zh_ is None else zh_
        b = core if core_ is None else core_
        c = zl if zl_ is None else zl_
        d = y if y_ is None else y_
        e = x if x_ is None else x_
        return (a * 2 + b, c * 16 + d * 4 + e)

    barrier = pltpu.get_barrier_semaphore()

    def greet(target):
        pl.semaphore_signal(barrier, inc=1, device_id=target, device_id_type=MESH)

    for n in range(1, 16):
        p = (y * 4 + x + n) % 16
        greet(dev(y_=p // 4, x_=p % 4))
    for n in range(1, 8):
        p = (zh * 2 + zl + n) % 8
        greet(dev(zh_=p // 2, zl_=p % 2))
    greet(dev(core_=1 - core))

    head = pltpu.make_async_copy(z_hbm.at[:, pl.ds(0, 16), :], zv.at[:, pl.ds(0, 16), :], z_sem.at[0])
    rest = pltpu.make_async_copy(z_hbm.at[:, pl.ds(16, 48), :], zv.at[:, pl.ds(16, 48), :], z_sem.at[1])
    head.start()
    rest.start()

    gin, bias_in = gin_ref[...].reshape(1, 128), bin_ref[...].reshape(1, 128)
    for n, w in enumerate((wlg_ref, wlp_ref, wrg_ref, wrp_ref)):
        wt[n * 128 : (n + 1) * 128, :] = w[...].astype(F32).T.astype(BF16)
    gain_c[...] = jnp.broadcast_to(gout_ref[...].reshape(1, 128), (128, 128)).T
    bias_c[...] = jnp.broadcast_to(bout_ref[...].reshape(1, 128), (128, 128)).T

    head.wait()

    def widen(b, _):
        i0 = pl.multiple_of(b * 8, 8)
        v = zv[pl.ds(i0, 8), 0:16, :].astype(F32)
        for i in range(8):
            zf[pl.ds((i0 + i) * 9, 8), :] = v[i, 0:8]
        return 0

    lax.fori_loop(0, 32, widen, 0, unroll=4)

    def norm_window(k, _):
        v = zf[pl.ds(k, 256, stride=9), :].astype(BF16)
        normed_w[k] = norm_rows(v, gin, bias_in)
        return 0

    lax.fori_loop(0, NK, norm_window, 0, unroll=6)

    def project(k, part):
        return lax.dot_general(
            wt[part * 256 : part * 256 + 256, :], normed_w[k], (((1,), (1,)), ((), ())), preferred_element_type=F32
        )

    def window_left(k, _):
        both = project(k, 0)
        left = (jax.nn.sigmoid(both[0:128]) * both[128:256]).astype(BF16)
        for h in range(2):
            for ab in range(2):
                pair = (y * 4 + x) if ab == 0 else (x * 4 + y)
                panel[h, ab, pair, zl * NK + k] = left[ab * 64 : ab * 64 + 64, h * 128 : h * 128 + 128]
        return 0

    low = lax.broadcasted_iota(jnp.int32, (32, 128), 1) < 64

    def window_right(k, _):
        both = project(k, 1)
        right = jax.nn.sigmoid(both[0:128]) * both[128:256]
        for u in range(2):
            for ab in range(2):
                lo = right[ab * 64 : ab * 64 + 32, u * 128 : u * 128 + 128]
                hi = right[ab * 64 + 32 : ab * 64 + 64, u * 128 : u * 128 + 128]
                r_send[2 * u, k, ab * 32 : ab * 32 + 32, :] = jnp.where(low, lo, pltpu.roll(hi, 64, 1)).astype(BF16)
                r_send[2 * u + 1, k, ab * 32 : ab * 32 + 32, :] = jnp.where(low, pltpu.roll(lo, 64, 1), hi).astype(BF16)
        return 0

    lax.fori_loop(0, NK, window_right, 0, unroll=6)
    pl.semaphore_wait(barrier, 23)

    copies = {}

    def left_copy(name, ref, target):
        if name not in copies:
            copies[name] = len(copies), ref, target
        left_made(name).start()

    def left_made(name):
        n, ref, target = copies[name]
        return pltpu.make_async_remote_copy(
            src_ref=ref(), dst_ref=ref(), send_sem=send_sem.at[n], recv_sem=recv_sem.at[n], device_id=target(),
            device_id_type=MESH,
        )

    def arrived(name, ref):
        n = copies[name][0]
        pltpu.make_async_copy(ref, ref, recv_sem.at[n]).wait()

    def first(ab):
        return x if ab == 0 else y

    def second(ab):
        return y if ab == 0 else x

    def step_first(ab, d):
        return dev(x_=(x + d) % 4) if ab == 0 else dev(y_=(y + d) % 4)

    def step_second(ab, d):
        return dev(y_=(y + d) % 4) if ab == 0 else dev(x_=(x + d) % 4)

    def pair_ref(h, ab, ds, df, half=None):
        p = ((second(ab) + ds) % 4) * 4 + (first(ab) + df) % 4
        if half is None:
            return panel.at[h, ab, p]
        return panel.at[h, ab, p, :, pl.ds(half * 32, 32), :]

    def z_ref(h, ab, z):
        return panel.at[h, ab, second(ab) * 4 + first(ab), pl.ds(z * NK, NK)]

    def send_z(h):
        for ab in range(2):
            left_copy(("z", h, ab), partial(z_ref, h, ab, zl), partial(dev, zl_=1 - zl))

    def wait_z(h):
        for ab in range(2):
            arrived(("z", h, ab), z_ref(h, ab, 1 - zl))

    def send_p1(h):
        for ab in range(2):
            for d in (1, -1):
                left_copy(("p1", h, ab, d), partial(pair_ref, h, ab, 0, 0), partial(step_first, ab, d))

    def send_q1(h, df):
        for ab in range(2):
            for d in (1, -1):
                left_copy(("q1", h, ab, df, d), partial(pair_ref, h, ab, 0, df), partial(step_second, ab, d))

    def pass_p1(h):
        for d in (1, -1):
            for ab in range(2):
                arrived(("p1", h, ab, d), pair_ref(h, ab, 0, -d))
                half = 0 if d == 1 else 1
                left_copy(("p2", h, ab, d), partial(pair_ref, h, ab, 0, -d, half), partial(step_first, ab, d))

    def wait_p2(h):
        for d in (1, -1):
            for ab in range(2):
                half = 0 if d == 1 else 1
                arrived(("p2", h, ab, d), pair_ref(h, ab, 0, 2, half))

    def pass_q1(h, df):
        for d in (1, -1):
            for ab in range(2):
                arrived(("q1", h, ab, df, d), pair_ref(h, ab, -d, df))
                half = 0 if d == 1 else 1
                left_copy(("q2", h, ab, df, d), partial(pair_ref, h, ab, -d, df, half), partial(step_second, ab, d))

    def wait_q2(h, df):
        for d in (1, -1):
            for ab in range(2):
                half = 0 if d == 1 else 1
                arrived(("q2", h, ab, df, d), pair_ref(h, ab, 2, df, half))

    own_slot = y * 4 + x
    ty = row % 4
    gathers = jnp.logical_and(y // 2 == zh % 2, core == y % 2)
    relays = core == y % 2

    def r1_ref(ref, n, ab):
        return ref.at[n, :, pl.ds(ab * 32, 32), :]

    def r1_copy(q, ab):
        return pltpu.make_async_remote_copy(
            src_ref=r1_ref(r_send, q, ab), dst_ref=r1_ref(r_gather, own_slot, ab),
            send_sem=r1_send.at[q * 2 + ab], recv_sem=r1_recv.at[ab], device_id=dev(y_=ty, x_=q), device_id_type=MESH,
        )

    def r1_mine(q):
        return jnp.logical_and(ty == y, x == q)

    def start_r1():
        for ab in range(2):
            for q in range(4):
                @pl.when(r1_mine(q))
                def _():
                    pltpu.make_async_copy(r1_ref(r_send, q, ab), r1_ref(r_gather, own_slot, ab), r1_recv.at[ab]).start()

                @pl.when(jnp.logical_not(r1_mine(q)))
                def _():
                    r1_copy(q, ab).start()

    def piece(ref, p):
        return ref.at[:, :, pl.ds(p * 16, 16), :]

    def r2_copy(p, o):
        return pltpu.make_async_remote_copy(
            src_ref=piece(r_gather, p), dst_ref=piece(r_nat.at[zl], p), send_sem=r2_send.at[p * 4 + o],
            recv_sem=r2_recv.at[p * 2 + zl], device_id=dev(zh_=(zh + o) % 4, zl_=zh // 2), device_id_type=MESH,
        )

    at_home = zl == zh // 2

    def start_r2(ab):
        @pl.when(gathers)
        def _():
            got = r_gather.at[:, :, pl.ds(ab * 32, 32), :]
            pltpu.make_async_copy(got, got, r1_recv.at[ab]).wait()
            for p in (2 * ab, 2 * ab + 1):
                r2_copy(p, 1).start()
                r2_copy(p, 3).start()

                @pl.when(at_home)
                def _():
                    pltpu.make_async_copy(piece(r_gather, p), piece(r_nat.at[zl], p), r2_recv.at[p * 2 + zl]).start()

                @pl.when(jnp.logical_not(at_home))
                def _():
                    r2_copy(p, 0).start()

    rel = (zh + 4 - (2 * zl + y // 2)) % 4

    def far_ref(p, z, half):
        return r_nat.at[z, pl.ds(half * 8, 8), :, pl.ds(p * 16, 16), :]

    def far_copy(p, z, half):
        return pltpu.make_async_remote_copy(
            src_ref=far_ref(p, z, half), dst_ref=far_ref(p, z, half), send_sem=rf_send.at[p * 2 + z],
            recv_sem=rf_recv.at[p * 4 + z * 2 + half],
            device_id=dev(zh_=(zh + (1 if half == 0 else 3)) % 4), device_id_type=MESH,
        )

    def r3_copy(p, z):
        part = piece(r_nat.at[z], p)
        return pltpu.make_async_remote_copy(
            src_ref=part, dst_ref=part, send_sem=r3_send.at[p * 2 + z], recv_sem=r3_recv.at[p * 2 + z],
            device_id=dev(core_=1 - core), device_id_type=MESH,
        )

    def pass_r2(p):
        @pl.when(jnp.logical_and(relays, rel != 2))
        def _():
            for z in range(2):
                part = piece(r_nat.at[z], p)
                pltpu.make_async_copy(part, part, r2_recv.at[p * 2 + z]).wait()
                for half in range(2):
                    @pl.when(rel == 1 + 2 * half)
                    def _():
                        far_copy(p, z, half).start()
                r3_copy(p, z).start()

    def wait_right(p):
        @pl.when(jnp.logical_and(relays, rel == 2))
        def _():
            for z in range(2):
                for half in range(2):
                    part = far_ref(p, z, half)
                    pltpu.make_async_copy(part, part, rf_recv.at[p * 4 + z * 2 + half]).wait()
                r3_copy(p, z).start()

        @pl.when(jnp.logical_not(relays))
        def _():
            for z in range(2):
                part = piece(r_nat.at[z], p)
                pltpu.make_async_copy(part, part, r3_recv.at[p * 2 + z]).wait()

    def gate_part(lo, hi):
        def body(b, _):
            i0 = pl.multiple_of(b * 16, 16)
            normed = norm_rows(zv[pl.ds(i0, 16)].reshape(1024, 128), gin, bias_in)
            g = jax.nn.sigmoid(jnp.dot(normed, wog_ref[...], preferred_element_type=F32))
            zv[pl.ds(i0, 16)] = g.astype(BF16).reshape(16, 64, 128)
            return 0

        lax.fori_loop(lo // 4, hi // 4, body, 0)

    def prep_right(p):
        ab = p // 2

        def relay(s, _):
            for f in range(4):
                slot_ = (s * 4 + f) if ab == 0 else (f * 4 + s)
                for z in range(2):
                    for k in range(NK):
                        zf[pl.ds(s * 48 + f * 12 + z * NK + k, 16, stride=193), :] = r_nat[
                            z, slot_, k, p * 16 : p * 16 + 16, :
                        ].astype(F32)
            return 0

        lax.fori_loop(0, 4, relay, 0)

        def turn(c, _):
            m = zf[pl.ds(c * 193, 192), :]
            r_mat[p * 16 + c] = m.astype(BF16).T
            return 0

        lax.fori_loop(0, 16, turn, 0, unroll=4)

    def relayout(h, ds):
        for ab in range(2):
            s = (second(ab) + ds) % 4

            def relay(f, _):
                for k in range(2 * NK):
                    rows = pl.ds(f * 12 + k, 64, stride=49)
                    swap[ab, rows, :] = panel[h, ab, s * 4 + f, k].astype(F32)
                return 0

            lax.fori_loop(0, 4, relay, 0)

            def pack(c, _):
                v = swap[ab, pl.ds(c * 49, 48), :]
                lefts[h, ab * 64 + c, pl.ds(pl.multiple_of(s * 48, 16), 48), :] = v.astype(BF16)
                return 0

            lax.fori_loop(0, 64, pack, 0, unroll=8)

    def multiply(h, p):
        def mul(n, total):
            c2 = p * 16 + n
            for cp in range(2):
                c = (p // 2) * 64 + cp * 32 + (p % 2) * 16 + n
                part = jnp.dot(r_mat[c2, cp * 64 : cp * 64 + 64, :], lefts[h, c], preferred_element_type=F32)
                acc[pl.ds(c * 65, 64), :] = part
                total = total + part
            return total

        start = jnp.zeros((64, 128), F32) if p == 0 else sums[...]
        sums[...] = lax.fori_loop(0, 16, mul, start, unroll=8)

    def normalise_product():
        mean = sums[...] * (1.0 / 128)

        def square(c, total):
            centred = acc[pl.ds(c * 65, 64), :] - mean
            return total + centred * centred

        spread = lax.fori_loop(0, 128, square, jnp.zeros((64, 128), F32), unroll=8)
        scale = lax.rsqrt(spread * (1.0 / 128) + 1e-05)

        def normalise(c, _):
            rows = pl.ds(c * 65, 64)
            acc[rows, :] = (acc[rows, :] - mean) * scale * gain_c[pl.ds(c, 1), :] + bias_c[pl.ds(c, 1), :]
            return 0

        lax.fori_loop(0, 128, normalise, 0, unroll=8)

    def finish(h):
        def columns(b, _):
            turned = [acc[pl.ds(b * 4 + n, 128, stride=65), :].astype(BF16).T for n in range(4)]
            result = jnp.dot(jnp.concatenate(turned, axis=0), wo_ref[...], preferred_element_type=F32)
            for n in range(4):
                proj[pl.ds(b * 4 + n, 128, stride=65), :] = result[n * 128 : n * 128 + 128]
            return 0

        lax.fori_loop(0, 16, columns, 0, unroll=2)

        for part in range(4):
            def body(i, _):
                g = zv[h * 128 + i].astype(F32)
                v = g * proj[pl.ds(i * 65, 64), :]
                zv[h * 128 + i] = v.astype(BF16)
                return 0

            lax.fori_loop(part * 32, part * 32 + 32, body, 0, unroll=8)
            out_copy(h, part).start()

    def out_copy(h, part):
        rows = pl.ds(h * 128 + part * 32, 32)
        return pltpu.make_async_copy(zv.at[rows], out_hbm.at[rows], out_sem.at[h * 4 + part])

    start_r1()
    lax.fori_loop(0, NK, window_left, 0, unroll=6)
    send_z(0)
    send_z(1)
    rest.wait()
    gate_part(0, 4)
    wait_z(0)
    send_p1(0)
    send_q1(0, 0)
    gate_part(4, 8)
    start_r2(0)
    gate_part(8, 12)
    pass_p1(0)
    send_q1(0, -1)
    send_q1(0, 1)
    start_r2(1)
    gate_part(12, 20)
    pass_q1(0, 0)
    wait_p2(0)
    send_q1(0, 2)
    gate_part(20, 28)
    wait_z(1)
    send_p1(1)
    relayout(0, 0)
    gate_part(28, 36)
    pass_q1(0, -1)
    pass_q1(0, 1)
    send_q1(1, 0)
    gate_part(36, 44)
    pass_r2(0)
    gate_part(44, 48)
    pass_q1(0, 2)
    pass_p1(1)
    send_q1(1, -1)
    send_q1(1, 1)
    gate_part(48, 56)
    pass_r2(1)
    gate_part(56, 64)
    relayout(0, -1)
    pass_q1(1, 0)
    wait_p2(1)
    send_q1(1, 2)
    pass_r2(2)
    relayout(0, 1)
    pass_r2(3)
    for df in DF:
        wait_q2(0, df)
    relayout(0, 2)
    pass_q1(1, -1)
    pass_q1(1, 1)
    for p in range(2):
        wait_right(p)
        prep_right(p)
        multiply(0, p)
    relayout(1, 0)
    wait_right(2)
    prep_right(2)
    multiply(0, 2)

    @pl.when(rel == 2)
    def _():
        pass_q1(1, 2)

    wait_right(3)
    prep_right(3)
    multiply(0, 3)
    normalise_product()

    @pl.when(rel != 2)
    def _():
        pass_q1(1, 2)

    finish(0)
    relayout(1, -1)
    relayout(1, 1)
    for df in DF:
        wait_q2(1, df)
    relayout(1, 2)
    for p in range(4):
        multiply(1, p)
    normalise_product()
    finish(1)

    for name in copies:
        left_made(name).wait_send()
    for q in range(4):
        @pl.when(jnp.logical_not(r1_mine(q)))
        def _():
            for ab in range(2):
                r1_copy(q, ab).wait_send()

    @pl.when(gathers)
    def _():
        for p in range(4):
            r2_copy(p, 1).wait_send()
            r2_copy(p, 3).wait_send()

        @pl.when(jnp.logical_not(at_home))
        def _():
            for p in range(4):
                r2_copy(p, 0).wait_send()

    @pl.when(relays)
    def _():
        for p in range(4):
            for z in range(2):
                for half in range(2):
                    @pl.when(rel == 1 + 2 * half)
                    def _():
                        far_copy(p, z, half).wait_send()
                r3_copy(p, z).wait_send()

    for h in range(2):
        for part in range(4):
            out_copy(h, part).wait()


def body(*args):
    vmem = pl.BlockSpec(memory_space=pltpu.VMEM)
    anywhere = pl.BlockSpec(memory_space=pl.ANY)
    return pl.pallas_call(
        kernel,
        out_shape=jax.ShapeDtypeStruct((256, 64, 128), BF16),
        in_specs=[anywhere] + [vmem] * 10,
        out_specs=anywhere,
        scratch_shapes=[
            pltpu.VMEM((256, 64, 128), BF16),
            pltpu.VMEM((3104, 128), F32),
            pltpu.VMEM((512, 128), BF16),
            pltpu.VMEM((NK, 256, 128), BF16),
            pltpu.VMEM((2, 2, 16, 12, 64, 128), BF16),
            pltpu.VMEM((4, NK, 64, 128), BF16),
            pltpu.VMEM((16, NK, 64, 128), BF16),
            pltpu.VMEM((2, 16, NK, 64, 128), BF16),
            pltpu.VMEM((64, 128, 192), BF16),
            pltpu.VMEM((2, 128, 192, 128), BF16),
            pltpu.VMEM((2, 64 * 49, 128), F32),
            pltpu.VMEM((128 * 65, 128), F32),
            pltpu.VMEM((64, 128), F32),
            pltpu.VMEM((128 * 65, 128), F32),
            pltpu.VMEM((128, 128), F32),
            pltpu.VMEM((128, 128), F32),
            pltpu.SemaphoreType.DMA((2,)),
            pltpu.SemaphoreType.DMA((8,)),
            pltpu.SemaphoreType.DMA((N_COPIES,)),
            pltpu.SemaphoreType.DMA((N_COPIES,)),
            pltpu.SemaphoreType.DMA((8,)),
            pltpu.SemaphoreType.DMA((2,)),
            pltpu.SemaphoreType.DMA((16,)),
            pltpu.SemaphoreType.DMA((8,)),
            pltpu.SemaphoreType.DMA((8,)),
            pltpu.SemaphoreType.DMA((16,)),
            pltpu.SemaphoreType.DMA((8,)),
            pltpu.SemaphoreType.DMA((8,)),
        ],
        compiler_params=pltpu.CompilerParams(
            collective_id=0, has_side_effects=True, vmem_limit_bytes=60 * 1024 * 1024
        ),
        cost_estimate=pl.CostEstimate(flops=2_000_000_000, bytes_accessed=8_400_000, transcendentals=2_000_000),
    )(*args)


def solution(mesh):
    in_specs = (P("row", "col", None),) + (P(),) * 10
    return jax.shard_map(body, mesh=mesh, in_specs=in_specs, out_specs=P("row", "col", None), check_vma=False)
```
